32 devices in a mesh: dp: 4 (over y, x), ctx: 8 (over z, core).
Axes of the slice: x: 2, y: 2, z: 4, core: 2. Of those that a mesh axis runs over, the one named last changes fastest.
Arguments:
- normed_layer_input: bfloat16 [4, 1024, 8192], P('dp', 'ctx'), may hold values from -6 to 6
- frozen_query_rows: bfloat16 [4, 1024, 2048], P('dp', 'ctx'), may hold values from -160 to 160
- projected_keys: bfloat16 [4, 1024, 256], P('dp', 'ctx'), may hold values from -7 to 7
- projected_values: bfloat16 [4, 1024, 256], P('dp', 'ctx'), may hold values from -6 to 6
- output_gradient: bfloat16 [4, 1024, 2048], P('dp', 'ctx'), may hold values from -6 to 6
- adapter_down: bfloat16 [8192, 16], replicated, may hold values from -0.0625 to 0.0625
- adapter_up: bfloat16 [16, 2048], replicated, may hold values from -1.5 to 1.5
- langevin_down_noise: float32 [8192, 16], replicated, may hold values from -1.8 to 1.8
- langevin_up_noise: float32 [16, 2048], replicated, may hold values from -0.6 to 0.6
- listed_key_blocks: int32 [16, 8, 12], replicated, may hold values from 0 to 7, as said below
- head_live_slots: int32 [16], replicated, may hold values from 4 to 12, as said below
Outputs:
- attention: bfloat16 [4, 1024, 2048], P('dp', 'ctx')
- step_down: float32 [8192, 16], replicated
- step_up: float32 [16, 2048], replicated
The draws below stay inside these ranges and needn't reach their ends.
Inputs may be any that keep to these rules, and one draw needn't show every extreme that they name: `listed_key_blocks`: slot 0 of block b's list is b, slot 1 is b - 1, slot 2 is b + 1 (modulo 8), slot 3 is block 0, for every head; the other slots are any blocks. `head_live_slots`: each count is a multiple of 4.
All inputs are finite; a program needn't handle non-finite values.
Results may differ from the reference program's by a relative error of at most 0.013.
Values may be sent and summed in bfloat16 or wider, within the bound.
A program may use at most 128 MiB of HBM per device.

```python
import jax
import jax.numpy as jnp
from jax import lax

MODEL_WIDTH = 8192
HEAD_SIZE = 128
ADAPTER_RANK = 16
G = 8
BLK = 128
NBMAX = 12
QUERY_HEAD_COUNT = 16
KVH = 2
DOCS = 4
SEQ = 1024
NQB = 8


def draw_head_live_slots(key, part):
    order_perm = jax.random.permutation(jax.random.fold_in(key, 11), QUERY_HEAD_COUNT)
    position = jnp.argsort(order_perm)
    levels = 4 * jax.random.randint(jax.random.fold_in(key, 12), (QUERY_HEAD_COUNT,), 1, NBMAX // 4 + 1)
    levels = jnp.where(position == 0, 4, levels)
    levels = jnp.where(position == 1, NBMAX, levels)
    return levels.astype(jnp.int32)


def draw_listed_key_blocks(key, part):
    blocks = jnp.arange(NQB, dtype=jnp.int32)
    fixed_slots = jnp.stack([blocks, (blocks - 1) % NQB, (blocks + 1) % NQB, jnp.zeros_like(blocks)], axis=1)
    fixed_slots = jnp.broadcast_to(fixed_slots[None], (QUERY_HEAD_COUNT, NQB, 4))
    random_slots = jax.random.randint(jax.random.fold_in(key, 31), (QUERY_HEAD_COUNT, NQB, NBMAX - 4), 0, NQB)
    return jnp.concatenate([fixed_slots, random_slots.astype(jnp.int32)], axis=2).astype(jnp.int32)


def key_field(key):
    field_values = jnp.clip(jax.random.normal(jax.random.fold_in(key, 21), (DOCS, SEQ, KVH * HEAD_SIZE), jnp.float32), -6.0, 6.0)
    return field_values


def draw_projected_keys(key, part):
    return key_field(key).astype(jnp.bfloat16)


def draw_frozen_query_rows(key, part):
    base_values = jnp.clip(jax.random.normal(jax.random.fold_in(key, 23), (DOCS, SEQ, QUERY_HEAD_COUNT * HEAD_SIZE), jnp.float32), -6.0, 6.0)
    return base_values.astype(jnp.bfloat16)


def steps_of(own_key, dims, cuts, least, high):
    def one(dim, shards_of):
        heights = jax.random.uniform(jax.random.fold_in(jax.random.fold_in(own_key, 6), dim), (shards_of,), jnp.float32, least / len(cuts), high / len(cuts))
        return jnp.repeat(jnp.exp(heights), dims[dim] // shards_of).reshape((-1,) + (1,) * (len(dims) - dim - 1))

    loudness = one(*cuts[0])
    for cut in cuts[1:]:
        loudness = loudness * one(*cut)
    return loudness


def noise(own_key, shape, deviation, bound, split=(), kind=jnp.bfloat16):
    gain = steps_of(own_key, shape, split, -0.22, 0.18) if split else 1.0
    drawn = jax.random.normal(own_key, shape, jnp.float32) * deviation * gain
    return jnp.minimum(jnp.maximum(drawn, -bound), bound).astype(kind)


def setup_inputs(seed: int = 0) -> dict:
    keys = jax.random.split(jax.random.key(seed), 12)
    normed_layer_input = noise(keys[0], (DOCS, SEQ, MODEL_WIDTH), 1.0, 6.0, ((0, 4), (1, 8)))
    frozen_query_rows = draw_frozen_query_rows(jax.random.fold_in(keys[11], 71), 0)
    projected_keys = draw_projected_keys(jax.random.fold_in(keys[11], 71), 0)
    projected_values = noise(keys[3], (DOCS, SEQ, KVH * HEAD_SIZE), 1.0, 6.0, ((0, 4), (1, 8)))
    output_gradient = noise(keys[4], (DOCS, SEQ, QUERY_HEAD_COUNT * HEAD_SIZE), 1.0, 6.0, ((0, 4), (1, 8)))
    adapter_down = noise(keys[5], (MODEL_WIDTH, ADAPTER_RANK), MODEL_WIDTH ** -0.5, 0.0625)
    adapter_up = noise(keys[6], (ADAPTER_RANK, QUERY_HEAD_COUNT * HEAD_SIZE), ADAPTER_RANK ** -0.5, 1.5)
    langevin_down_noise = noise(keys[7], (MODEL_WIDTH, ADAPTER_RANK), 0.3, 1.8, (), jnp.float32)
    langevin_up_noise = noise(keys[8], (ADAPTER_RANK, QUERY_HEAD_COUNT * HEAD_SIZE), 0.1, 0.6, (), jnp.float32)
    listed_key_blocks = draw_listed_key_blocks(jax.random.fold_in(keys[11], 71), 0)
    head_live_slots = draw_head_live_slots(jax.random.fold_in(keys[11], 71), 0)
    return dict(normed_layer_input=normed_layer_input, frozen_query_rows=frozen_query_rows, projected_keys=projected_keys, projected_values=projected_values, output_gradient=output_gradient, adapter_down=adapter_down, adapter_up=adapter_up, langevin_down_noise=langevin_down_noise, langevin_up_noise=langevin_up_noise, listed_key_blocks=listed_key_blocks, head_live_slots=head_live_slots)


ADAPTER_GAIN = 2.0
MASK_VALUE = -1.0e30


def attend(queries, cotangent, key_rows, value_rows, live_mask):
    scaling = queries.shape[-1] ** -0.5
    scores = jnp.einsum("gqd,gkd->gqk", queries.astype(jnp.float32), key_rows.astype(jnp.float32)) * scaling
    scores = jnp.where(live_mask[:, None, :], scores, MASK_VALUE)
    largest = jnp.max(scores, axis=-1, keepdims=True)
    shifted = jnp.exp(scores - largest)
    weights = shifted / jnp.sum(shifted, axis=-1, keepdims=True)
    weights_low = weights.astype(jnp.bfloat16)
    outputs = jnp.einsum("gqk,gkd->gqd", weights_low.astype(jnp.float32), value_rows.astype(jnp.float32)).astype(jnp.bfloat16)
    weight_grad = jnp.einsum("gqd,gkd->gqk", cotangent.astype(jnp.float32), value_rows.astype(jnp.float32))
    row_inner = jnp.sum(weights * weight_grad, axis=-1, keepdims=True)
    score_grad = (weights * (weight_grad - row_inner)).astype(jnp.bfloat16)
    query_gradient = (jnp.einsum("gqk,gkd->gqd", score_grad.astype(jnp.float32), key_rows.astype(jnp.float32)) * scaling).astype(jnp.bfloat16)
    return outputs, query_gradient


def block_pass(query_blocks, grad_blocks, key_blocks, value_blocks, slot_lists, live_mask, per_step):
    block_total = query_blocks.shape[0]
    slot_count = slot_lists.shape[1]

    def grouped(tensor):
        return tensor.reshape((block_total // per_step, per_step) + tensor.shape[1:])

    def step_fn(pieces):
        query_part, grad_part, list_part, mask_part = pieces
        key_rows = key_blocks[list_part].reshape(per_step, slot_count * BLK, HEAD_SIZE)
        value_rows = value_blocks[list_part].reshape(per_step, slot_count * BLK, HEAD_SIZE)
        return attend(query_part, grad_part, key_rows, value_rows, mask_part)

    outputs, grads = lax.map(step_fn, (grouped(query_blocks), grouped(grad_blocks), grouped(slot_lists), grouped(live_mask)))
    return outputs.reshape(query_blocks.shape), grads.reshape(query_blocks.shape)


def one_head(query_head, grad_head, key_head, value_head, slot_lists, live_count):
    block_total = slot_lists.shape[0]
    per_step = min(block_total, max(1, 512 // BLK))
    live_row = (jnp.arange(NBMAX * BLK, dtype=jnp.int32) // BLK) < live_count
    live_mask = jnp.broadcast_to(live_row[None, :], (block_total, NBMAX * BLK))
    outputs, grads = block_pass(query_head.reshape(block_total, BLK, HEAD_SIZE), grad_head.reshape(block_total, BLK, HEAD_SIZE),
                                key_head.reshape(block_total, BLK, HEAD_SIZE), value_head.reshape(block_total, BLK, HEAD_SIZE),
                                slot_lists, live_mask, per_step)
    return outputs.reshape(block_total * BLK, HEAD_SIZE), grads.reshape(block_total * BLK, HEAD_SIZE)


def reference(normed_layer_input, frozen_query_rows, projected_keys, projected_values, output_gradient, adapter_down, adapter_up, langevin_down_noise, langevin_up_noise, listed_key_blocks, head_live_slots):
    live_slots = head_live_slots.astype(jnp.int32)
    group_of = jnp.arange(QUERY_HEAD_COUNT, dtype=jnp.int32) // G
    grad_down = jnp.zeros((MODEL_WIDTH, ADAPTER_RANK), jnp.float32)
    up_gradient = jnp.zeros((ADAPTER_RANK, QUERY_HEAD_COUNT * HEAD_SIZE), jnp.float32)
    outputs_all = []
    for document_text in range(DOCS):
        reduced_rank_rows = jnp.dot(normed_layer_input[document_text], adapter_down, preferred_element_type=jnp.float32).astype(jnp.bfloat16)
        query_matrix = (frozen_query_rows[document_text].astype(jnp.float32) + ADAPTER_GAIN * jnp.dot(reduced_rank_rows, adapter_up, preferred_element_type=jnp.float32)).astype(jnp.bfloat16)
        query_heads = query_matrix.reshape(SEQ, QUERY_HEAD_COUNT, HEAD_SIZE).transpose(1, 0, 2)
        grad_heads = output_gradient[document_text].reshape(SEQ, QUERY_HEAD_COUNT, HEAD_SIZE).transpose(1, 0, 2)
        key_heads = projected_keys[document_text].reshape(SEQ, KVH, HEAD_SIZE).transpose(1, 0, 2)
        value_heads = projected_values[document_text].reshape(SEQ, KVH, HEAD_SIZE).transpose(1, 0, 2)

        def per_head(pieces):
            query_head, grad_head, slot_lists, group_index, live_count = pieces
            return one_head(query_head, grad_head, key_heads[group_index], value_heads[group_index], slot_lists, live_count)

        head_out, head_grad = lax.map(per_head, (query_heads, grad_heads, listed_key_blocks, group_of, live_slots))
        attended = head_out.transpose(1, 0, 2).reshape(SEQ, QUERY_HEAD_COUNT * HEAD_SIZE)
        query_gradient = head_grad.transpose(1, 0, 2).reshape(SEQ, QUERY_HEAD_COUNT * HEAD_SIZE)
        up_gradient = up_gradient + ADAPTER_GAIN * jnp.dot(reduced_rank_rows.T, query_gradient, preferred_element_type=jnp.float32)
        reduced_gradient = (ADAPTER_GAIN * jnp.dot(query_gradient, adapter_up.T, preferred_element_type=jnp.float32)).astype(jnp.bfloat16)
        grad_down = grad_down + jnp.dot(normed_layer_input[document_text].T, reduced_gradient, preferred_element_type=jnp.float32)
        outputs_all.append(attended)
    token_norm = (DOCS * SEQ) ** -0.5
    return jnp.stack(outputs_all), grad_down * token_norm + langevin_down_noise, up_gradient * token_norm + langevin_up_noise
```

```python
import functools

import jax
import jax.numpy as jnp
from jax import lax
from jax.experimental import pallas as pl
from jax.experimental.pallas import tpu as pltpu
from jax.sharding import PartitionSpec as P

HEAD_SIZE = 128
G = 8
BLK = 128
ADAPTER_GAIN = 2.0
MASK_VALUE = -1e30
LOG2E = 1.4426950408889634
MESH = pl.DeviceIdType.MESH
F32 = jnp.float32
BF16 = jnp.bfloat16


def dot_nt(a, b):
    return lax.dot_general(a, b, (((1,), (1,)), ((), ())), preferred_element_type=F32)


def dot_tn(a, b):
    return lax.dot_general(a, b, (((0,), (0,)), ((), ())), preferred_element_type=F32)


def dot_nn(a, b):
    return jnp.dot(a, b, preferred_element_type=F32)


def kernel(
    ndp,
    nctx,
    per_step,
    x_hbm,
    frozen_hbm,
    k_hbm,
    v_hbm,
    og_hbm,
    down_t,
    up,
    lists,
    live,
    att_out,
    tot_down,
    tot_up,
    x,
    frozen,
    og,
    kv,
    q,
    qg,
    bias,
    gbuf,
    rbuf,
    zbuf,
    abuf,
    load_sem,
    z_send,
    z_recv,
    c_send,
    c_recv,
    rs_send,
    rs_recv,
    gz_send,
    gz_recv,
    ag_send,
    ag_recv,
):
    dp, ctx = lax.axis_index("dp"), lax.axis_index("ctx")
    nz, na = nctx // 2, ndp * 2
    z, core = lax.div(ctx, 2), lax.rem(ctx, 2)
    a = dp * 2 + core
    kvw = k_hbm.shape[1]
    width = x.shape[1]
    qw = q.shape[1]
    heads = qw // HEAD_SIZE
    wd, wu = width // na, qw // na
    keys = nctx * BLK

    def rows_of(c):
        return pl.ds(pl.multiple_of(c * BLK, BLK), BLK)

    def plane_id(k):
        p = lax.rem(a + k, na)
        return p, (lax.div(p, 2), z * 2 + lax.rem(p, 2))

    def line_id(k):
        return (dp, lax.rem(z + k, nz) * 2 + core)

    loads = []
    for i, (src, dst) in enumerate(
        (
            (k_hbm, kv.at[rows_of(ctx), pl.ds(0, kvw)]),
            (v_hbm, kv.at[rows_of(ctx), pl.ds(kvw, kvw)]),
            (x_hbm, x),
            (frozen_hbm, frozen),
            (og_hbm, og),
        )
    ):
        copy = pltpu.make_async_copy(src, dst, load_sem.at[i])
        copy.start()
        loads.append(copy)

    barrier = pltpu.get_barrier_semaphore()
    for k in range(1, na):
        pl.semaphore_signal(barrier, inc=1, device_id=plane_id(k)[1], device_id_type=MESH)
    for k in range(1, nz):
        pl.semaphore_signal(barrier, inc=1, device_id=line_id(k), device_id_type=MESH)
    pl.semaphore_wait(barrier, na - 1 + nz - 1)

    loads[0].wait()
    loads[1].wait()
    sibling = (dp, z * 2 + 1 - core)
    line_copies = []
    for k in range(1, nz):
        copy = pltpu.make_async_remote_copy(
            src_ref=kv.at[rows_of(ctx), :],
            dst_ref=kv.at[rows_of(ctx), :],
            send_sem=z_send.at[k],
            recv_sem=z_recv.at[k],
            device_id=line_id(k),
            device_id_type=MESH,
        )
        copy.start()
        line_copies.append(copy)

    def to_sibling(k):
        rows = rows_of(lax.rem(z - k + nz, nz) * 2 + core)
        copy = pltpu.make_async_remote_copy(
            src_ref=kv.at[rows, :],
            dst_ref=kv.at[rows, :],
            send_sem=c_send.at[k],
            recv_sem=c_recv.at[k],
            device_id=sibling,
            device_id_type=MESH,
        )
        copy.start()
        return copy

    core_copies = [to_sibling(0)]

    nqb, slots = lists.shape[1], lists.shape[2]
    mine = lax.broadcasted_iota(jnp.int32, lists.shape, 1) == ctx
    local = jnp.sum(jnp.where(mine, lists[...].astype(F32), 0.0), axis=1)
    head_iota = lax.broadcasted_iota(jnp.int32, (heads, 1), 0)
    live_col = jnp.zeros((heads, 1), jnp.int32)
    for h in range(heads):
        live_col = jnp.where(head_iota == h, live[h], live_col)
    slot_iota = lax.broadcasted_iota(jnp.int32, (heads, slots), 1)
    local = jnp.where(slot_iota < live_col, local, -1.0)
    block_of = (lax.broadcasted_iota(jnp.int32, (heads, keys), 1) // BLK).astype(F32)
    count = jnp.zeros((heads, keys), F32)
    for j in range(slots):
        count += jnp.where(block_of == local[:, j : j + 1], 1.0, 0.0)
    bias[...] = jnp.where(count > 0.0, jnp.log(jnp.maximum(count, 1.0)) * LOG2E, MASK_VALUE)

    loads[2].wait()
    low_rank = dot_nt(x[...], down_t[...]).astype(BF16)
    loads[3].wait()
    q[...] = (frozen[...].astype(F32) + ADAPTER_GAIN * dot_nn(low_rank, up[...])).astype(BF16)

    for k in range(1, nz):
        line_copies[k - 1].wait_recv()
        core_copies.append(to_sibling(k))
    for copy in core_copies:
        copy.wait_recv()
    loads[4].wait()

    scaling = HEAD_SIZE ** (-0.5)

    def one_head(h):
        group = h // G
        cols = pl.ds(pl.multiple_of(h * HEAD_SIZE, HEAD_SIZE), HEAD_SIZE)
        kcols = pl.ds(pl.multiple_of(group * HEAD_SIZE, HEAD_SIZE), HEAD_SIZE)
        vcols = pl.ds(pl.multiple_of(kvw + group * HEAD_SIZE, HEAD_SIZE), HEAD_SIZE)
        key_rows, value_rows = kv[:, kcols], kv[:, vcols]
        scores = dot_nt(q[:, cols], key_rows) * (scaling * LOG2E) + bias[pl.ds(h, 1), :]
        weights = jnp.exp2(scores - jnp.max(scores, axis=-1, keepdims=True))
        weight_grad = dot_nt(og[:, cols], value_rows)
        inverse = 1.0 / jnp.sum(weights, axis=-1, keepdims=True)
        inner = jnp.sum(weights * weight_grad, axis=-1, keepdims=True) * inverse
        score_grad = (weights * (weight_grad - inner)).astype(BF16)
        att_out[:, cols] = (dot_nn(weights.astype(BF16), value_rows) * inverse).astype(BF16)
        qg[:, cols] = (dot_nn(score_grad, key_rows) * (inverse * scaling)).astype(BF16)

    def head_step(i, carry):
        for j in range(per_step):
            one_head(i * per_step + j)
        return carry

    lax.fori_loop(0, heads // per_step, head_step, 0)

    low_grad = (ADAPTER_GAIN * dot_nt(qg[...], up[...])).astype(BF16)

    def chunk(p):
        dcols = pl.ds(pl.multiple_of(p * wd, 128), wd)
        ucols = pl.ds(pl.multiple_of(p * wu, 128), wu)
        return dot_tn(low_grad, x[:, dcols]), ADAPTER_GAIN * dot_tn(low_rank, qg[:, ucols])

    rs_copies = []
    for k in range(1, na):
        p, device = plane_id(k)
        part_down, part_up = chunk(p)
        gbuf[k, :, :wd] = part_down.astype(BF16)
        gbuf[k, :, wd:] = part_up.astype(BF16)
        copy = pltpu.make_async_remote_copy(
            src_ref=gbuf.at[k],
            dst_ref=rbuf.at[k],
            send_sem=rs_send.at[k],
            recv_sem=rs_recv.at[k],
            device_id=device,
            device_id_type=MESH,
        )
        copy.start()
        rs_copies.append(copy)
    sum_down, sum_up = chunk(a)
    for k in range(1, na):
        rs_copies[k - 1].wait_recv()
        sum_down += rbuf[k, :, :wd].astype(F32)
        sum_up += rbuf[k, :, wd:].astype(F32)
    zbuf[z, :, :wd] = sum_down.astype(BF16)
    zbuf[z, :, wd:] = sum_up.astype(BF16)

    gz_copies = []
    for k in range(1, nz):
        copy = pltpu.make_async_remote_copy(
            src_ref=zbuf.at[z],
            dst_ref=zbuf.at[z],
            send_sem=gz_send.at[k],
            recv_sem=gz_recv.at[k],
            device_id=line_id(k),
            device_id_type=MESH,
        )
        copy.start()
        gz_copies.append(copy)
    for copy in gz_copies:
        copy.wait_recv()
    total = zbuf[0].astype(F32)
    for i in range(1, nz):
        total += zbuf[i].astype(F32)
    abuf[a] = total.astype(BF16)

    ag_copies = []
    for k in range(1, na):
        copy = pltpu.make_async_remote_copy(
            src_ref=abuf.at[a],
            dst_ref=abuf.at[a],
            send_sem=ag_send.at[k],
            recv_sem=ag_recv.at[k],
            device_id=plane_id(k)[1],
            device_id_type=MESH,
        )
        copy.start()
        ag_copies.append(copy)
    for copy in line_copies + core_copies + rs_copies + gz_copies:
        copy.wait_send()
    for copy in ag_copies:
        copy.wait()
    for p in range(na):
        tot_down[:, p * wd : (p + 1) * wd] = abuf[p, :, :wd]
        tot_up[:, p * wu : (p + 1) * wu] = abuf[p, :, wd:]


def body(
    ndp,
    nctx,
    normed_layer_input,
    frozen_query_rows,
    projected_keys,
    projected_values,
    output_gradient,
    adapter_down,
    adapter_up,
    langevin_down_noise,
    langevin_up_noise,
    listed_key_blocks,
    head_live_slots,
):
    tok, width = normed_layer_input.shape[1:]
    qw, kvw = frozen_query_rows.shape[2], projected_keys.shape[2]
    rank = adapter_up.shape[0]
    heads = qw // HEAD_SIZE
    keys = nctx * tok
    nz, na = nctx // 2, ndp * 2
    piece = (width + qw) // na
    per_step = 2 if keys <= 1024 else 1
    any_spec = pl.BlockSpec(memory_space=pl.ANY)
    vmem_spec = pl.BlockSpec(memory_space=pltpu.VMEM)
    smem_spec = pl.BlockSpec(memory_space=pltpu.SMEM)
    dma = pltpu.SemaphoreType.DMA
    attended, total_down, total_up = pl.pallas_call(
        functools.partial(kernel, ndp, nctx, per_step),
        out_shape=(
            jax.ShapeDtypeStruct((tok, qw), BF16),
            jax.ShapeDtypeStruct((rank, width), BF16),
            jax.ShapeDtypeStruct((rank, qw), BF16),
        ),
        in_specs=[any_spec] * 5 + [vmem_spec] * 3 + [smem_spec],
        out_specs=(vmem_spec, vmem_spec, vmem_spec),
        scratch_shapes=[
            pltpu.VMEM((tok, width), BF16),
            pltpu.VMEM((tok, qw), BF16),
            pltpu.VMEM((tok, qw), BF16),
            pltpu.VMEM((keys, 2 * kvw), BF16),
            pltpu.VMEM((tok, qw), BF16),
            pltpu.VMEM((tok, qw), BF16),
            pltpu.VMEM((heads, keys), F32),
            pltpu.VMEM((na, rank, piece), BF16),
            pltpu.VMEM((na, rank, piece), BF16),
            pltpu.VMEM((nz, rank, piece), BF16),
            pltpu.VMEM((na, rank, piece), BF16),
            dma((5,)),
            dma((nz,)),
            dma((nz,)),
            dma((nz,)),
            dma((nz,)),
            dma((na,)),
            dma((na,)),
            dma((nz,)),
            dma((nz,)),
            dma((na,)),
            dma((na,)),
        ],
        compiler_params=pltpu.CompilerParams(
            collective_id=0, has_side_effects=True, vmem_limit_bytes=56 * 2**20
        ),
        name="adapter_attention",
    )(
        normed_layer_input[0],
        frozen_query_rows[0],
        projected_keys[0],
        projected_values[0],
        output_gradient[0],
        adapter_down.T,
        adapter_up,
        listed_key_blocks,
        head_live_slots,
    )
    token_norm = (tok * nctx * ndp) ** (-0.5)
    return (
        attended[None],
        total_down.T.astype(F32) * token_norm + langevin_down_noise,
        total_up.astype(F32) * token_norm + langevin_up_noise,
    )


def solution(mesh):
    rows = P("dp", "ctx", None)
    return jax.shard_map(
        functools.partial(body, mesh.shape["dp"], mesh.shape["ctx"]),
        mesh=mesh,
        in_specs=(rows,) * 5 + (P(),) * 6,
        out_specs=(rows, P(), P()),
        check_vma=False,
    )
```

```python
import functools

import jax
import jax.numpy as jnp
from jax import lax
from jax.experimental import pallas as pl
from jax.experimental.pallas import tpu as pltpu
from jax.sharding import PartitionSpec as P

HEAD_SIZE = 128
G = 8
BLK = 128
ADAPTER_GAIN = 2.0
MASK_VALUE = -1e30
LOG2E = 1.4426950408889634
MESH = pl.DeviceIdType.MESH
F32 = jnp.float32
BF16 = jnp.bfloat16


def dot_nt(a, b):
    return lax.dot_general(a, b, (((1,), (1,)), ((), ())), preferred_element_type=F32)


def dot_tn(a, b):
    return lax.dot_general(a, b, (((0,), (0,)), ((), ())), preferred_element_type=F32)


def dot_nn(a, b):
    return jnp.dot(a, b, preferred_element_type=F32)


def kernel(
    ndp,
    nctx,
    per_step,
    early,
    x_hbm,
    frozen_hbm,
    k_hbm,
    v_hbm,
    og_hbm,
    noise_down_hbm,
    noise_up_hbm,
    down_t,
    up,
    lists,
    live,
    att_hbm,
    step_down_hbm,
    step_up_hbm,
    x,
    frozen,
    og,
    kv,
    q,
    qg,
    att,
    step_down,
    step_up,
    bias,
    scores_buf,
    grads_buf,
    gbuf,
    rbuf,
    zbuf,
    abuf,
    load_sem,
    store_sem,
    z_send,
    z_recv,
    c_send,
    c_recv,
    rs_send,
    rs_recv,
    gz_send,
    gz_recv,
    ag_send,
    ag_recv,
):
    dp, ctx = lax.axis_index("dp"), lax.axis_index("ctx")
    nz, na = nctx // 2, ndp * 2
    z, core = lax.div(ctx, 2), lax.rem(ctx, 2)
    a = dp * 2 + core
    kvw = k_hbm.shape[1]
    width = x.shape[1]
    qw = q.shape[1]
    heads = qw // HEAD_SIZE
    wd, wu = width // na, qw // na
    keys = nctx * BLK

    own_rows = pl.ds(pl.multiple_of(core * BLK, BLK), BLK)

    def line(k):
        if nz & (nz - 1):
            return lax.rem(z + nz - k, nz)
        other, bit = z, 1
        while bit < nz:
            if k & bit:
                other = other + bit * (1 - 2 * lax.rem(lax.div(z, bit), 2))
            bit *= 2
        return other

    def plane_id(k):
        p = lax.rem(a + k, na)
        return p, (lax.div(p, 2), z * 2 + lax.rem(p, 2))

    def line_id(k):
        to = lax.rem(z + k, nz) if nz & (nz - 1) else line(k)
        return (dp, to * 2 + core)

    loads = []
    for i, (src, dst) in enumerate(
        (
            (k_hbm, kv.at[0, own_rows, pl.ds(0, kvw)]),
            (v_hbm, kv.at[0, own_rows, pl.ds(kvw, kvw)]),
            (x_hbm, x),
            (frozen_hbm, frozen),
            (og_hbm, og),
            (noise_down_hbm, step_down),
            (noise_up_hbm, step_up),
        )
    ):
        copy = pltpu.make_async_copy(src, dst, load_sem.at[i])
        copy.start()
        loads.append(copy)

    barrier = pltpu.get_barrier_semaphore()
    for k in range(1, na):
        pl.semaphore_signal(barrier, inc=1, device_id=plane_id(k)[1], device_id_type=MESH)
    for k in range(1, nz):
        pl.semaphore_signal(barrier, inc=1, device_id=line_id(k), device_id_type=MESH)
    pl.semaphore_wait(barrier, na - 1 + nz - 1)

    loads[0].wait()
    loads[1].wait()
    sibling = (dp, z * 2 + 1 - core)
    line_copies = []
    for k in range(1, nz):
        copy = pltpu.make_async_remote_copy(
            src_ref=kv.at[0, own_rows, :],
            dst_ref=kv.at[k, own_rows, :],
            send_sem=z_send.at[k],
            recv_sem=z_recv.at[k],
            device_id=line_id(k),
            device_id_type=MESH,
        )
        copy.start()
        line_copies.append(copy)

    def to_sibling(k):
        copy = pltpu.make_async_remote_copy(
            src_ref=kv.at[k, own_rows, :],
            dst_ref=kv.at[k, own_rows, :],
            send_sem=c_send.at[k],
            recv_sem=c_recv.at[k],
            device_id=sibling,
            device_id_type=MESH,
        )
        copy.start()
        return copy

    core_copies = [to_sibling(0)]

    slots, nqb = lists.shape[:2]
    mine = lax.broadcasted_iota(jnp.int32, lists.shape, 1) == ctx
    local = jnp.sum(jnp.where(mine, lists[...].astype(F32), 0.0), axis=1)
    head_iota = lax.broadcasted_iota(jnp.int32, (1, heads), 1)
    live_row = jnp.zeros((1, heads), jnp.int32)
    for h in range(heads):
        live_row = jnp.where(head_iota == h, live[h], live_row)
    block_iota = lax.broadcasted_iota(jnp.int32, (nqb, heads), 0).astype(F32)
    count = jnp.zeros((nqb, heads), F32)
    for j in range(slots):
        listed = jnp.where(live_row > j, local[j : j + 1, :], -1.0)
        count += jnp.where(block_iota == listed, 1.0, 0.0)
    lane = lax.broadcasted_iota(jnp.int32, (1, keys), 1)
    held = jnp.zeros((1, keys), jnp.int32)
    for k in range(nz):
        held = jnp.where(lane // (2 * BLK) == k, line(k) * 2, held)
    held += (lane // BLK) % 2
    spread = jnp.where(lax.broadcasted_iota(jnp.int32, (nqb, keys), 0) == held, 1.0, 0.0)
    count = dot_tn(count, spread)
    bias[...] = jnp.where(count > 0.5, jnp.log(jnp.maximum(count, 1.0)) * LOG2E, MASK_VALUE)

    loads[2].wait()
    low_rank = dot_nt(x[...], down_t[...]).astype(BF16)
    loads[3].wait()
    q[...] = (frozen[...].astype(F32) + ADAPTER_GAIN * dot_nn(low_rank, up[...])).astype(BF16)

    loads[4].wait()
    scaling = HEAD_SIZE ** (-0.5)
    pair = 2 * BLK

    def stacked(ref, first, number):
        return jnp.concatenate(
            [
                ref[:, pl.ds(pl.multiple_of((first + j) * HEAD_SIZE, HEAD_SIZE), HEAD_SIZE)]
                for j in range(number)
            ],
            axis=0,
        )

    def scores_of(k):
        def group_step(group, carry):
            kcols = pl.ds(pl.multiple_of(group * HEAD_SIZE, HEAD_SIZE), HEAD_SIZE)
            vcols = pl.ds(pl.multiple_of(kvw + group * HEAD_SIZE, HEAD_SIZE), HEAD_SIZE)
            rows = pl.ds(pl.multiple_of(group * G * BLK, G * BLK), G * BLK)
            scores_buf[k, rows, :] = dot_nt(stacked(q, group * G, G), kv[k, :, kcols])
            grads_buf[k, rows, :] = dot_nt(stacked(og, group * G, G), kv[k, :, vcols])
            return carry

        lax.fori_loop(0, heads // G, group_step, 0)

    for k in range(nz):
        if k > 0:
            line_copies[k - 1].wait_recv()
            core_copies.append(to_sibling(k))
        if early:
            core_copies[k].wait_recv()
            scores_of(k)
    if not early:
        for copy in core_copies:
            copy.wait_recv()

    def head_step(i, carry):
        first = i * per_step
        group = first // G
        kcols = pl.ds(pl.multiple_of(group * HEAD_SIZE, HEAD_SIZE), HEAD_SIZE)
        vcols = pl.ds(pl.multiple_of(kvw + group * HEAD_SIZE, HEAD_SIZE), HEAD_SIZE)
        key_rows = kv[:, :, kcols].reshape(keys, HEAD_SIZE)
        value_rows = kv[:, :, vcols].reshape(keys, HEAD_SIZE)
        all_weights, all_grads, all_inverse = [], [], []
        for j in range(per_step):
            h = first + j
            if early:
                rows = pl.ds(pl.multiple_of(h * BLK, BLK), BLK)
                scores = jnp.concatenate([scores_buf[k, rows, :] for k in range(nz)], axis=1)
                weight_grad = jnp.concatenate([grads_buf[k, rows, :] for k in range(nz)], axis=1)
            else:
                cols = pl.ds(pl.multiple_of(h * HEAD_SIZE, HEAD_SIZE), HEAD_SIZE)
                scores = dot_nt(q[:, cols], key_rows)
                weight_grad = dot_nt(og[:, cols], value_rows)
            scores = scores * (scaling * LOG2E) + bias[pl.ds(h, 1), :]
            weights = jnp.exp2(scores - jnp.max(scores, axis=-1, keepdims=True))
            inverse = 1.0 / jnp.sum(weights, axis=-1, keepdims=True)
            inner = jnp.sum(weights * weight_grad, axis=-1, keepdims=True) * inverse
            all_weights.append(weights.astype(BF16))
            all_grads.append((weights * (weight_grad - inner)).astype(BF16))
            all_inverse.append(inverse)
        attended = dot_nn(jnp.concatenate(all_weights, axis=0), value_rows)
        query_grad = dot_nn(jnp.concatenate(all_grads, axis=0), key_rows)
        for j in range(per_step):
            cols = pl.ds(pl.multiple_of((first + j) * HEAD_SIZE, HEAD_SIZE), HEAD_SIZE)
            rows = slice(j * BLK, (j + 1) * BLK)
            att[:, cols] = (attended[rows] * all_inverse[j]).astype(BF16)
            qg[:, cols] = (query_grad[rows] * (all_inverse[j] * scaling)).astype(BF16)
        return carry

    lax.fori_loop(0, heads // per_step, head_step, 0)
    att_store = pltpu.make_async_copy(att, att_hbm, store_sem.at[0])
    att_store.start()

    low_grad = (ADAPTER_GAIN * dot_nt(qg[...], up[...])).astype(BF16)

    def chunk(p):
        dcols = pl.ds(pl.multiple_of(p * wd, 128), wd)
        ucols = pl.ds(pl.multiple_of(p * wu, 128), wu)
        return dot_tn(low_grad, x[:, dcols]), ADAPTER_GAIN * dot_tn(low_rank, qg[:, ucols])

    rs_copies = []
    for k in range(1, na):
        p, device = plane_id(k)
        part_down, part_up = chunk(p)
        gbuf[k, :, :wd] = part_down.astype(BF16)
        gbuf[k, :, wd:] = part_up.astype(BF16)
        copy = pltpu.make_async_remote_copy(
            src_ref=gbuf.at[k],
            dst_ref=rbuf.at[k],
            send_sem=rs_send.at[k],
            recv_sem=rs_recv.at[k],
            device_id=device,
            device_id_type=MESH,
        )
        copy.start()
        rs_copies.append(copy)
    sum_down, sum_up = chunk(a)
    for k in range(1, na):
        rs_copies[k - 1].wait_recv()
        sum_down += rbuf[k, :, :wd].astype(F32)
        sum_up += rbuf[k, :, wd:].astype(F32)
    zbuf[z, :, :wd] = sum_down.astype(BF16)
    zbuf[z, :, wd:] = sum_up.astype(BF16)

    gz_copies = []
    for k in range(1, nz):
        copy = pltpu.make_async_remote_copy(
            src_ref=zbuf.at[z],
            dst_ref=zbuf.at[z],
            send_sem=gz_send.at[k],
            recv_sem=gz_recv.at[k],
            device_id=line_id(k),
            device_id_type=MESH,
        )
        copy.start()
        gz_copies.append(copy)
    for copy in gz_copies:
        copy.wait_recv()
    total = zbuf[0].astype(F32)
    for i in range(1, nz):
        total += zbuf[i].astype(F32)
    abuf[a] = total.astype(BF16)

    ag_copies = []
    for k in range(1, na):
        copy = pltpu.make_async_remote_copy(
            src_ref=abuf.at[a],
            dst_ref=abuf.at[a],
            send_sem=ag_send.at[k],
            recv_sem=ag_recv.at[k],
            device_id=plane_id(k)[1],
            device_id_type=MESH,
        )
        copy.start()
        ag_copies.append(copy)
    for copy in line_copies + core_copies + rs_copies + gz_copies:
        copy.wait_send()
    loads[5].wait()
    loads[6].wait()
    for copy in ag_copies:
        copy.wait()
    norm = (BLK * nctx * ndp) ** (-0.5)
    for p in range(na):
        step_down[:, p * wd : (p + 1) * wd] += abuf[p, :, :wd].astype(F32) * norm
        step_up[:, p * wu : (p + 1) * wu] += abuf[p, :, wd:].astype(F32) * norm
    stores = [
        pltpu.make_async_copy(step_down, step_down_hbm, store_sem.at[1]),
        pltpu.make_async_copy(step_up, step_up_hbm, store_sem.at[2]),
    ]
    for copy in stores:
        copy.start()
    for copy in [att_store] + stores:
        copy.wait()


def hand_over(*refs):
    sem = refs[-1]
    copies = []
    for i in range(3):
        rows = refs[i].shape[0] // 2
        for j in range(2):
            part = pl.ds(j * rows, rows)
            copies.append(
                pltpu.make_async_copy(refs[i].at[part], refs[3 + i].at[part], sem.at[2 * i + j])
            )
    for copy in copies:
        copy.start()
    for copy in copies:
        copy.wait()


def body(
    ndp,
    nctx,
    normed_layer_input,
    frozen_query_rows,
    projected_keys,
    projected_values,
    output_gradient,
    adapter_down,
    adapter_up,
    langevin_down_noise,
    langevin_up_noise,
    listed_key_blocks,
    head_live_slots,
):
    tok, width = normed_layer_input.shape[1:]
    qw, kvw = frozen_query_rows.shape[2], projected_keys.shape[2]
    rank = adapter_up.shape[0]
    heads = qw // HEAD_SIZE
    keys = nctx * tok
    nz, na = nctx // 2, ndp * 2
    piece = (width + qw) // na
    early = 2 * heads * tok * keys * 4 <= 2**24
    per_step = 4 if early else 1
    any_spec = pl.BlockSpec(memory_space=pl.ANY)
    vmem_spec = pl.BlockSpec(memory_space=pltpu.VMEM)
    smem_spec = pl.BlockSpec(memory_space=pltpu.SMEM)
    dma = pltpu.SemaphoreType.DMA
    held_scores = (nz, heads * tok, 2 * BLK) if early else (1, 8, 128)
    results = (
        jax.ShapeDtypeStruct((tok, qw), BF16),
        jax.ShapeDtypeStruct((rank, width), F32),
        jax.ShapeDtypeStruct((rank, qw), F32),
    )
    outputs = pl.pallas_call(
        functools.partial(kernel, ndp, nctx, per_step, early),
        out_shape=results,
        in_specs=[any_spec] * 7 + [vmem_spec] * 3 + [smem_spec],
        out_specs=(any_spec,) * 3,
        scratch_shapes=[
            pltpu.VMEM((tok, width), BF16),
            pltpu.VMEM((tok, qw), BF16),
            pltpu.VMEM((tok, qw), BF16),
            pltpu.VMEM((nz, 2 * BLK, 2 * kvw), BF16),
            pltpu.VMEM((tok, qw), BF16),
            pltpu.VMEM((tok, qw), BF16),
            pltpu.VMEM((tok, qw), BF16),
            pltpu.VMEM((rank, width), F32),
            pltpu.VMEM((rank, qw), F32),
            pltpu.VMEM((heads, keys), F32),
            pltpu.VMEM(held_scores, F32),
            pltpu.VMEM(held_scores, F32),
            pltpu.VMEM((na, rank, piece), BF16),
            pltpu.VMEM((na, rank, piece), BF16),
            pltpu.VMEM((nz, rank, piece), BF16),
            pltpu.VMEM((na, rank, piece), BF16),
            dma((7,)),
            dma((3,)),
            dma((nz,)),
            dma((nz,)),
            dma((nz,)),
            dma((nz,)),
            dma((na,)),
            dma((na,)),
            dma((nz,)),
            dma((nz,)),
            dma((na,)),
            dma((na,)),
        ],
        compiler_params=pltpu.CompilerParams(
            collective_id=0,
            has_side_effects=True,
            vmem_limit_bytes=60 * 2**20,
        ),
        name="adapter_attention",
    )(
        normed_layer_input[0],
        frozen_query_rows[0],
        projected_keys[0],
        projected_values[0],
        output_gradient[0],
        langevin_down_noise.T,
        langevin_up_noise,
        adapter_down.T,
        adapter_up,
        listed_key_blocks.transpose(2, 1, 0),
        head_live_slots,
    )
    attended, step_down, step_up = pl.pallas_call(
        hand_over,
        out_shape=results,
        in_specs=[any_spec] * 3,
        out_specs=(any_spec,) * 3,
        scratch_shapes=[dma((6,))],
        name="hand_over",
    )(*outputs)
    return attended[None], step_down.T, step_up


def solution(mesh):
    rows = P("dp", "ctx", None)
    return jax.shard_map(
        functools.partial(body, mesh.shape["dp"], mesh.shape["ctx"]),
        mesh=mesh,
        in_specs=(rows,) * 5 + (P(),) * 6,
        out_specs=(rows, P(), P()),
        check_vma=False,
    )
```

```python
import functools

import jax
import jax.numpy as jnp
from jax import lax
from jax.experimental import pallas as pl
from jax.experimental.pallas import tpu as pltpu
from jax.sharding import PartitionSpec as P

HEAD_SIZE = 128
G = 8
BLK = 128
ADAPTER_GAIN = 2.0
MASK_VALUE = -1e30
LOG2E = 1.4426950408889634
MESH = pl.DeviceIdType.MESH
F32 = jnp.float32
BF16 = jnp.bfloat16


def dot_nt(a, b):
    return lax.dot_general(a, b, (((1,), (1,)), ((), ())), preferred_element_type=F32)


def dot_tn(a, b):
    return lax.dot_general(a, b, (((0,), (0,)), ((), ())), preferred_element_type=F32)


def dot_nn(a, b):
    return jnp.dot(a, b, preferred_element_type=F32)


def kernel(
    ndp,
    nctx,
    per_step,
    early,
    x_hbm,
    frozen_hbm,
    k_hbm,
    v_hbm,
    og_hbm,
    noise_down_hbm,
    noise_up_hbm,
    down_t,
    up,
    lists,
    live,
    att_hbm,
    step_down_hbm,
    step_up_hbm,
    x,
    frozen,
    og,
    kv,
    q,
    qg,
    att,
    step_down,
    step_up,
    bias,
    weights_buf,
    grads_buf,
    sums_buf,
    tops_buf,
    gbuf,
    rbuf,
    zbuf,
    abuf,
    load_sem,
    store_sem,
    z_send,
    z_recv,
    c_send,
    c_recv,
    rs_send,
    rs_recv,
    gz_send,
    gz_recv,
    ag_send,
    ag_recv,
):
    dp, ctx = lax.axis_index("dp"), lax.axis_index("ctx")
    nz, na = nctx // 2, ndp * 2
    z, core = lax.div(ctx, 2), lax.rem(ctx, 2)
    a = dp * 2 + core
    kvw = k_hbm.shape[1]
    width = x.shape[1]
    qw = q.shape[1]
    heads = qw // HEAD_SIZE
    wd, wu = width // na, qw // na
    keys = nctx * BLK

    own_rows = pl.ds(pl.multiple_of(core * BLK, BLK), BLK)

    def line(k):
        if nz & (nz - 1):
            return lax.rem(z + nz - k, nz)
        other, bit = z, 1
        while bit < nz:
            if k & bit:
                other = other + bit * (1 - 2 * lax.rem(lax.div(z, bit), 2))
            bit *= 2
        return other

    def plane_id(k):
        p = lax.rem(a + k, na)
        return p, (lax.div(p, 2), z * 2 + lax.rem(p, 2))

    def line_id(k):
        to = lax.rem(z + k, nz) if nz & (nz - 1) else line(k)
        return (dp, to * 2 + core)

    loads = []
    for i, (src, dst) in enumerate(
        (
            (k_hbm, kv.at[0, own_rows, pl.ds(0, kvw)]),
            (v_hbm, kv.at[0, own_rows, pl.ds(kvw, kvw)]),
            (x_hbm, x),
            (frozen_hbm, frozen),
            (og_hbm, og),
            (noise_down_hbm, step_down),
            (noise_up_hbm, step_up),
        )
    ):
        copy = pltpu.make_async_copy(src, dst, load_sem.at[i])
        copy.start()
        loads.append(copy)

    barrier = pltpu.get_barrier_semaphore()
    for k in range(1, na):
        pl.semaphore_signal(barrier, inc=1, device_id=plane_id(k)[1], device_id_type=MESH)
    for k in range(1, nz):
        pl.semaphore_signal(barrier, inc=1, device_id=line_id(k), device_id_type=MESH)
    pl.semaphore_wait(barrier, na - 1 + nz - 1)

    loads[0].wait()
    loads[1].wait()
    sibling = (dp, z * 2 + 1 - core)
    line_copies = []
    for k in range(1, nz):
        copy = pltpu.make_async_remote_copy(
            src_ref=kv.at[0, own_rows, :],
            dst_ref=kv.at[k, own_rows, :],
            send_sem=z_send.at[k],
            recv_sem=z_recv.at[k],
            device_id=line_id(k),
            device_id_type=MESH,
        )
        copy.start()
        line_copies.append(copy)

    def to_sibling(k):
        copy = pltpu.make_async_remote_copy(
            src_ref=kv.at[k, own_rows, :],
            dst_ref=kv.at[k, own_rows, :],
            send_sem=c_send.at[k],
            recv_sem=c_recv.at[k],
            device_id=sibling,
            device_id_type=MESH,
        )
        copy.start()
        return copy

    core_copies = [to_sibling(0)]

    slots, nqb = lists.shape[:2]
    mine = lax.broadcasted_iota(jnp.int32, lists.shape, 1) == ctx
    local = jnp.sum(jnp.where(mine, lists[...].astype(F32), 0.0), axis=1)
    head_iota = lax.broadcasted_iota(jnp.int32, (1, heads), 1)
    live_row = jnp.zeros((1, heads), jnp.int32)
    for h in range(heads):
        live_row = jnp.where(head_iota == h, live[h], live_row)
    block_iota = lax.broadcasted_iota(jnp.int32, (nqb, heads), 0).astype(F32)
    count = jnp.zeros((nqb, heads), F32)
    for j in range(slots):
        listed = jnp.where(live_row > j, local[j : j + 1, :], -1.0)
        count += jnp.where(block_iota == listed, 1.0, 0.0)
    lane = lax.broadcasted_iota(jnp.int32, (1, keys), 1)
    held = jnp.zeros((1, keys), jnp.int32)
    for k in range(nz):
        held = jnp.where(lane // (2 * BLK) == k, line(k) * 2, held)
    held += (lane // BLK) % 2
    spread = jnp.where(lax.broadcasted_iota(jnp.int32, (nqb, keys), 0) == held, 1.0, 0.0)
    count = dot_tn(count, spread)
    bias[...] = jnp.where(count > 0.5, jnp.log(jnp.maximum(count, 1.0)) * LOG2E, MASK_VALUE)

    loads[2].wait()
    low_rank = dot_nt(x[...], down_t[...]).astype(BF16)
    loads[3].wait()
    q[...] = (frozen[...].astype(F32) + ADAPTER_GAIN * dot_nn(low_rank, up[...])).astype(BF16)

    loads[4].wait()
    scaling = HEAD_SIZE ** (-0.5)
    pair = 2 * BLK

    def stacked(ref, first, number):
        return jnp.concatenate(
            [
                ref[:, pl.ds(pl.multiple_of((first + j) * HEAD_SIZE, HEAD_SIZE), HEAD_SIZE)]
                for j in range(number)
            ],
            axis=0,
        )

    def scores_of(k):
        def group_step(group, carry):
            kcols = pl.ds(pl.multiple_of(group * HEAD_SIZE, HEAD_SIZE), HEAD_SIZE)
            vcols = pl.ds(pl.multiple_of(kvw + group * HEAD_SIZE, HEAD_SIZE), HEAD_SIZE)
            rows = pl.ds(pl.multiple_of(group * G * BLK, G * BLK), G * BLK)
            scores = dot_nt(stacked(q, group * G, G), kv[k, :, kcols])
            grads_buf[k, rows, :] = dot_nt(stacked(og, group * G, G), kv[k, :, vcols])
            group_bias = bias[pl.ds(pl.multiple_of(group * G, G), G), k * pair : (k + 1) * pair]
            all_weights = []
            for j in range(G):
                head_rows = pl.ds(pl.multiple_of((group * G + j) * BLK, BLK), BLK)
                head_scores = scores[j * BLK : (j + 1) * BLK] * (scaling * LOG2E)
                head_scores += group_bias[j : j + 1]
                top = jnp.max(head_scores, axis=-1, keepdims=True)
                tops_buf[k, head_rows, :] = jnp.broadcast_to(top, (BLK, HEAD_SIZE))
                all_weights.append(jnp.exp2(head_scores - top).astype(BF16))
            weights = jnp.concatenate(all_weights, axis=0)
            weights_buf[k, rows, :] = weights
            values = jnp.concatenate([kv[k, :, vcols], jnp.ones((pair, HEAD_SIZE), BF16)], axis=1)
            sums_buf[k, rows, :] = dot_nn(weights, values)
            return carry

        lax.fori_loop(0, heads // G, group_step, 0)

    for k in range(nz):
        if k > 0:
            line_copies[k - 1].wait_recv()
            core_copies.append(to_sibling(k))
        if early:
            core_copies[k].wait_recv()
            scores_of(k)
    if not early:
        for copy in core_copies:
            copy.wait_recv()

    def finish_step(i, carry):
        first = i * per_step
        kcols = pl.ds(pl.multiple_of(first // G * HEAD_SIZE, HEAD_SIZE), HEAD_SIZE)
        score_grads = [[] for _ in range(nz)]
        factors, scales = [], []
        for j in range(per_step):
            rows = pl.ds(pl.multiple_of((first + j) * BLK, BLK), BLK)
            cols = pl.ds(pl.multiple_of((first + j) * HEAD_SIZE, HEAD_SIZE), HEAD_SIZE)
            tops = [tops_buf[k, rows, :] for k in range(nz)]
            top = functools.reduce(jnp.maximum, tops)
            factor = [jnp.exp2(t - top) for t in tops]
            attended, total = 0.0, 0.0
            for k in range(nz):
                attended += factor[k] * sums_buf[k, rows, :HEAD_SIZE]
                total += factor[k] * sums_buf[k, rows, HEAD_SIZE:]
            inverse = 1.0 / total
            attended = attended * inverse
            att[:, cols] = attended.astype(BF16)
            inner = jnp.sum(attended * og[:, cols].astype(F32), axis=-1, keepdims=True)
            for k in range(nz):
                weights = weights_buf[k, rows, :].astype(F32)
                score_grads[k].append((weights * (grads_buf[k, rows, :] - inner)).astype(BF16))
            factors.append(factor)
            scales.append(inverse * scaling)
        parts = [
            dot_nn(jnp.concatenate(score_grads[k], axis=0), kv[k, :, kcols]) for k in range(nz)
        ]
        for j in range(per_step):
            cols = pl.ds(pl.multiple_of((first + j) * HEAD_SIZE, HEAD_SIZE), HEAD_SIZE)
            query_grad = 0.0
            for k in range(nz):
                query_grad += factors[j][k] * parts[k][j * BLK : (j + 1) * BLK]
            qg[:, cols] = (query_grad * scales[j]).astype(BF16)
        return carry

    def head_step(i, carry):
        first = i * per_step
        group = first // G
        kcols = pl.ds(pl.multiple_of(group * HEAD_SIZE, HEAD_SIZE), HEAD_SIZE)
        vcols = pl.ds(pl.multiple_of(kvw + group * HEAD_SIZE, HEAD_SIZE), HEAD_SIZE)
        key_rows = kv[:, :, kcols].reshape(keys, HEAD_SIZE)
        value_rows = kv[:, :, vcols].reshape(keys, HEAD_SIZE)
        all_weights, all_grads, all_inverse = [], [], []
        for j in range(per_step):
            h = first + j
            cols = pl.ds(pl.multiple_of(h * HEAD_SIZE, HEAD_SIZE), HEAD_SIZE)
            scores = dot_nt(q[:, cols], key_rows)
            weight_grad = dot_nt(og[:, cols], value_rows)
            scores = scores * (scaling * LOG2E) + bias[pl.ds(h, 1), :]
            weights = jnp.exp2(scores - jnp.max(scores, axis=-1, keepdims=True))
            inverse = 1.0 / jnp.sum(weights, axis=-1, keepdims=True)
            inner = jnp.sum(weights * weight_grad, axis=-1, keepdims=True) * inverse
            all_weights.append(weights.astype(BF16))
            all_grads.append((weights * (weight_grad - inner)).astype(BF16))
            all_inverse.append(inverse)
        attended = dot_nn(jnp.concatenate(all_weights, axis=0), value_rows)
        query_grad = dot_nn(jnp.concatenate(all_grads, axis=0), key_rows)
        for j in range(per_step):
            cols = pl.ds(pl.multiple_of((first + j) * HEAD_SIZE, HEAD_SIZE), HEAD_SIZE)
            rows = slice(j * BLK, (j + 1) * BLK)
            att[:, cols] = (attended[rows] * all_inverse[j]).astype(BF16)
            qg[:, cols] = (query_grad[rows] * (all_inverse[j] * scaling)).astype(BF16)
        return carry

    lax.fori_loop(0, heads // per_step, finish_step if early else head_step, 0)
    att_store = pltpu.make_async_copy(att, att_hbm, store_sem.at[0])
    att_store.start()

    low_grad = (ADAPTER_GAIN * dot_nt(qg[...], up[...])).astype(BF16)

    def chunk(p):
        dcols = pl.ds(pl.multiple_of(p * wd, 128), wd)
        ucols = pl.ds(pl.multiple_of(p * wu, 128), wu)
        return dot_tn(low_grad, x[:, dcols]), ADAPTER_GAIN * dot_tn(low_rank, qg[:, ucols])

    rs_copies = []
    for k in range(1, na):
        p, device = plane_id(k)
        part_down, part_up = chunk(p)
        gbuf[k, :, :wd] = part_down.astype(BF16)
        gbuf[k, :, wd:] = part_up.astype(BF16)
        copy = pltpu.make_async_remote_copy(
            src_ref=gbuf.at[k],
            dst_ref=rbuf.at[k],
            send_sem=rs_send.at[k],
            recv_sem=rs_recv.at[k],
            device_id=device,
            device_id_type=MESH,
        )
        copy.start()
        rs_copies.append(copy)
    sum_down, sum_up = chunk(a)
    for k in range(1, na):
        rs_copies[k - 1].wait_recv()
        sum_down += rbuf[k, :, :wd].astype(F32)
        sum_up += rbuf[k, :, wd:].astype(F32)
    zbuf[z, :, :wd] = sum_down.astype(BF16)
    zbuf[z, :, wd:] = sum_up.astype(BF16)

    gz_copies = []
    for k in range(1, nz):
        copy = pltpu.make_async_remote_copy(
            src_ref=zbuf.at[z],
            dst_ref=zbuf.at[z],
            send_sem=gz_send.at[k],
            recv_sem=gz_recv.at[k],
            device_id=line_id(k),
            device_id_type=MESH,
        )
        copy.start()
        gz_copies.append(copy)
    for copy in gz_copies:
        copy.wait_recv()
    total = zbuf[0].astype(F32)
    for i in range(1, nz):
        total += zbuf[i].astype(F32)
    abuf[a] = total.astype(BF16)

    ag_copies = []
    for k in range(1, na):
        copy = pltpu.make_async_remote_copy(
            src_ref=abuf.at[a],
            dst_ref=abuf.at[a],
            send_sem=ag_send.at[k],
            recv_sem=ag_recv.at[k],
            device_id=plane_id(k)[1],
            device_id_type=MESH,
        )
        copy.start()
        ag_copies.append(copy)
    for copy in line_copies + core_copies + rs_copies + gz_copies:
        copy.wait_send()
    loads[5].wait()
    loads[6].wait()
    for copy in ag_copies:
        copy.wait()
    norm = (BLK * nctx * ndp) ** (-0.5)
    for p in range(na):
        step_down[:, p * wd : (p + 1) * wd] += abuf[p, :, :wd].astype(F32) * norm
        step_up[:, p * wu : (p + 1) * wu] += abuf[p, :, wd:].astype(F32) * norm
    stores = [
        pltpu.make_async_copy(step_down, step_down_hbm, store_sem.at[1]),
        pltpu.make_async_copy(step_up, step_up_hbm, store_sem.at[2]),
    ]
    for copy in stores:
        copy.start()
    for copy in [att_store] + stores:
        copy.wait()


def hand_over(*refs):
    sources, targets, held = refs[:3], refs[3:6], refs[6:9]
    in_sem, out_sem = refs[9:]
    first, second = [], []
    for i in range(3):
        rows = sources[i].shape[0] // 2
        for j in range(2):
            part, n = pl.ds(j * rows, rows), 2 * i + j
            first.append(
                pltpu.make_async_copy(sources[i].at[part], held[i].at[part], in_sem.at[n])
            )
            second.append(
                pltpu.make_async_copy(held[i].at[part], targets[i].at[part], out_sem.at[n])
            )
    for copy in first:
        copy.start()
    for arrive, leave in zip(first, second):
        arrive.wait()
        leave.start()
    for copy in second:
        copy.wait()


def body(
    ndp,
    nctx,
    normed_layer_input,
    frozen_query_rows,
    projected_keys,
    projected_values,
    output_gradient,
    adapter_down,
    adapter_up,
    langevin_down_noise,
    langevin_up_noise,
    listed_key_blocks,
    head_live_slots,
):
    tok, width = normed_layer_input.shape[1:]
    qw, kvw = frozen_query_rows.shape[2], projected_keys.shape[2]
    rank = adapter_up.shape[0]
    heads = qw // HEAD_SIZE
    keys = nctx * tok
    nz, na = nctx // 2, ndp * 2
    piece = (width + qw) // na
    early = 2 * heads * tok * keys * 4 <= 2**24
    per_step = 4 if early else 1
    any_spec = pl.BlockSpec(memory_space=pl.ANY)
    vmem_spec = pl.BlockSpec(memory_space=pltpu.VMEM)
    smem_spec = pl.BlockSpec(memory_space=pltpu.SMEM)
    dma = pltpu.SemaphoreType.DMA
    held_rows = (nz, heads * tok) if early else (1, 16)
    results = (
        jax.ShapeDtypeStruct((tok, qw), BF16),
        jax.ShapeDtypeStruct((rank, width), F32),
        jax.ShapeDtypeStruct((rank, qw), F32),
    )
    outputs = pl.pallas_call(
        functools.partial(kernel, ndp, nctx, per_step, early),
        out_shape=results,
        in_specs=[any_spec] * 7 + [vmem_spec] * 3 + [smem_spec],
        out_specs=(any_spec,) * 3,
        scratch_shapes=[
            pltpu.VMEM((tok, width), BF16),
            pltpu.VMEM((tok, qw), BF16),
            pltpu.VMEM((tok, qw), BF16),
            pltpu.VMEM((nz, 2 * BLK, 2 * kvw), BF16),
            pltpu.VMEM((tok, qw), BF16),
            pltpu.VMEM((tok, qw), BF16),
            pltpu.VMEM((tok, qw), BF16),
            pltpu.VMEM((rank, width), F32),
            pltpu.VMEM((rank, qw), F32),
            pltpu.VMEM((heads, keys), F32),
            pltpu.VMEM(held_rows + (2 * BLK,), BF16),
            pltpu.VMEM(held_rows + (2 * BLK,), F32),
            pltpu.VMEM(held_rows + (2 * HEAD_SIZE,), F32),
            pltpu.VMEM(held_rows + (HEAD_SIZE,), F32),
            pltpu.VMEM((na, rank, piece), BF16),
            pltpu.VMEM((na, rank, piece), BF16),
            pltpu.VMEM((nz, rank, piece), BF16),
            pltpu.VMEM((na, rank, piece), BF16),
            dma((7,)),
            dma((3,)),
            dma((nz,)),
            dma((nz,)),
            dma((nz,)),
            dma((nz,)),
            dma((na,)),
            dma((na,)),
            dma((nz,)),
            dma((nz,)),
            dma((na,)),
            dma((na,)),
        ],
        compiler_params=pltpu.CompilerParams(
            collective_id=0,
            has_side_effects=True,
            vmem_limit_bytes=60 * 2**20,
        ),
        name="adapter_attention",
    )(
        normed_layer_input[0],
        frozen_query_rows[0],
        projected_keys[0],
        projected_values[0],
        output_gradient[0],
        langevin_down_noise.T,
        langevin_up_noise,
        adapter_down.T,
        adapter_up,
        listed_key_blocks.transpose(2, 1, 0),
        head_live_slots,
    )
    attended, step_down, step_up = pl.pallas_call(
        hand_over,
        out_shape=results,
        in_specs=[any_spec] * 3,
        out_specs=(any_spec,) * 3,
        scratch_shapes=[pltpu.VMEM(r.shape, r.dtype) for r in results] + [dma((6,)), dma((6,))],
        compiler_params=pltpu.CompilerParams(vmem_limit_bytes=60 * 2**20),
        name="hand_over",
    )(*outputs)
    return attended[None], step_down.T, step_up


def solution(mesh):
    rows = P("dp", "ctx", None)
    return jax.shard_map(
        functools.partial(body, mesh.shape["dp"], mesh.shape["ctx"]),
        mesh=mesh,
        in_specs=(rows,) * 5 + (P(),) * 6,
        out_specs=(rows, P(), P()),
        check_vma=False,
    )
```

```python
import functools

import jax
import jax.numpy as jnp
from jax import lax
from jax.experimental import pallas as pl
from jax.experimental.pallas import tpu as pltpu
from jax.sharding import PartitionSpec as P

HEAD_SIZE = 128
G = 8
BLK = 128
ADAPTER_GAIN = 2.0
MASK_VALUE = -1e30
LOG2E = 1.4426950408889634
MESH = pl.DeviceIdType.MESH
F32 = jnp.float32
BF16 = jnp.bfloat16


def dot_nt(a, b):
    return lax.dot_general(a, b, (((1,), (1,)), ((), ())), preferred_element_type=F32)


def dot_tn(a, b):
    return lax.dot_general(a, b, (((0,), (0,)), ((), ())), preferred_element_type=F32)


def dot_nn(a, b):
    return jnp.dot(a, b, preferred_element_type=F32)


def send(source, target, send_sem, recv_sem, device):
    copy = pltpu.make_async_remote_copy(
        src_ref=source,
        dst_ref=target,
        send_sem=send_sem,
        recv_sem=recv_sem,
        device_id=device,
        device_id_type=MESH,
    )
    copy.start()
    return copy


def kernel(
    ndp,
    nctx,
    parts,
    per_step,
    early,
    x_hbm,
    frozen_hbm,
    k_hbm,
    v_hbm,
    og_hbm,
    noise_down_hbm,
    noise_up_hbm,
    down_t,
    up,
    lists,
    live,
    att_hbm,
    step_down_hbm,
    step_up_hbm,
    x,
    frozen,
    og,
    kv,
    q,
    qg,
    att,
    step_down,
    step_up,
    bias,
    weights_buf,
    grads_buf,
    sums_buf,
    tops_buf,
    sbuf,
    pbuf,
    gbuf,
    rbuf,
    zbuf,
    abuf,
    load_sem,
    store_sem,
    z_send,
    z_recv,
    c_send,
    c_recv,
    p_send,
    p_recv,
    rs_send,
    rs_recv,
    gz_send,
    gz_recv,
    ag_send,
    ag_recv,
    af_send,
    af_recv,
):
    dp, ctx = lax.axis_index("dp"), lax.axis_index("ctx")
    nz, na = nctx // 2, ndp * 2
    z, core = lax.div(ctx, 2), lax.rem(ctx, 2)
    kvw = k_hbm.shape[1]
    width = x.shape[1]
    qw = q.shape[1]
    heads = qw // HEAD_SIZE
    wd, wu = width // na, qw // na
    keys = nctx * BLK

    own_rows = pl.ds(pl.multiple_of(core * BLK, BLK), BLK)

    def line(k):
        if nz & (nz - 1):
            return lax.rem(z + nz - k, nz)
        other, bit = z, 1
        while bit < nz:
            if k & bit:
                other = other + bit * (1 - 2 * lax.rem(lax.div(z, bit), 2))
            bit *= 2
        return other

    sibling = (dp, z * 2 + 1 - core)

    def plane_id(k):
        return (lax.rem(dp + k, ndp), ctx)

    def line_id(k):
        to = lax.rem(z + k, nz) if nz & (nz - 1) else line(k)
        return (dp, to * 2 + core)

    loads = []
    for i, (src, dst) in enumerate(
        (
            (k_hbm, kv.at[0, own_rows, pl.ds(0, kvw)]),
            (v_hbm, kv.at[0, own_rows, pl.ds(kvw, kvw)]),
            (x_hbm, x),
            (frozen_hbm, frozen),
            (og_hbm, og),
            (noise_down_hbm, step_down),
            (noise_up_hbm, step_up),
        )
    ):
        copy = pltpu.make_async_copy(src, dst, load_sem.at[i])
        copy.start()
        loads.append(copy)

    barrier = pltpu.get_barrier_semaphore()
    partners = [sibling]
    partners += [plane_id(k) for k in range(1, ndp)]
    partners += [line_id(k) for k in range(1, nz)]
    for partner in partners:
        pl.semaphore_signal(barrier, inc=1, device_id=partner, device_id_type=MESH)

    slots, nqb = lists.shape[:2]
    mine = lax.broadcasted_iota(jnp.int32, lists.shape, 1) == ctx
    local = jnp.sum(jnp.where(mine, lists[...].astype(F32), 0.0), axis=1)
    head_iota = lax.broadcasted_iota(jnp.int32, (1, heads), 1)
    live_row = jnp.zeros((1, heads), jnp.int32)
    for h in range(heads):
        live_row = jnp.where(head_iota == h, live[h], live_row)
    block_iota = lax.broadcasted_iota(jnp.int32, (nqb, heads), 0).astype(F32)
    count = jnp.zeros((nqb, heads), F32)
    for j in range(slots):
        listed = jnp.where(live_row > j, local[j : j + 1, :], -1.0)
        count += jnp.where(block_iota == listed, 1.0, 0.0)
    lane = lax.broadcasted_iota(jnp.int32, (1, keys), 1)
    held = jnp.zeros((1, keys), jnp.int32)
    for k in range(nz):
        held = jnp.where(lane // (2 * BLK) == k, line(k) * 2, held)
    held += (lane // BLK) % 2
    spread = jnp.where(lax.broadcasted_iota(jnp.int32, (nqb, keys), 0) == held, 1.0, 0.0)
    count = dot_tn(count, spread)
    bias[...] = jnp.where(count > 0.5, jnp.log(jnp.maximum(count, 1.0)) * LOG2E, MASK_VALUE)

    pl.semaphore_wait(barrier, len(partners))

    loads[0].wait()
    loads[1].wait()
    line_copies = []
    for k in range(1, nz):
        source, target = kv.at[0, own_rows, :], kv.at[k, own_rows, :]
        line_copies.append(send(source, target, z_send.at[k], z_recv.at[k], line_id(k)))

    def to_sibling(k):
        rows = kv.at[k, own_rows, :]
        return send(rows, rows, c_send.at[k], c_recv.at[k], sibling)

    core_copies = [to_sibling(0)]

    loads[2].wait()
    low_rank = dot_nt(x[...], down_t[...]).astype(BF16)
    loads[3].wait()
    q[...] = (frozen[...].astype(F32) + ADAPTER_GAIN * dot_nn(low_rank, up[...])).astype(BF16)

    loads[4].wait()
    scaling = HEAD_SIZE ** (-0.5)
    pair = 2 * BLK

    def stacked(ref, first, number):
        return jnp.concatenate(
            [
                ref[:, pl.ds(pl.multiple_of((first + j) * HEAD_SIZE, HEAD_SIZE), HEAD_SIZE)]
                for j in range(number)
            ],
            axis=0,
        )

    def scores_of(k):
        def group_step(group, carry):
            kcols = pl.ds(pl.multiple_of(group * HEAD_SIZE, HEAD_SIZE), HEAD_SIZE)
            vcols = pl.ds(pl.multiple_of(kvw + group * HEAD_SIZE, HEAD_SIZE), HEAD_SIZE)
            rows = pl.ds(pl.multiple_of(group * G * BLK, G * BLK), G * BLK)
            scores = dot_nt(stacked(q, group * G, G), kv[k, :, kcols])
            grads_buf[k, rows, :] = dot_nt(stacked(og, group * G, G), kv[k, :, vcols])
            group_bias = bias[pl.ds(pl.multiple_of(group * G, G), G), k * pair : (k + 1) * pair]
            all_weights = []
            for j in range(G):
                head_rows = pl.ds(pl.multiple_of((group * G + j) * BLK, BLK), BLK)
                head_scores = scores[j * BLK : (j + 1) * BLK] * (scaling * LOG2E)
                head_scores += group_bias[j : j + 1]
                top = jnp.max(head_scores, axis=-1, keepdims=True)
                tops_buf[k, head_rows, :] = jnp.broadcast_to(top, (BLK, HEAD_SIZE))
                all_weights.append(jnp.exp2(head_scores - top).astype(BF16))
            weights = jnp.concatenate(all_weights, axis=0)
            weights_buf[k, rows, :] = weights
            values = jnp.concatenate([kv[k, :, vcols], jnp.ones((pair, HEAD_SIZE), BF16)], axis=1)
            sums_buf[k, rows, :] = dot_nn(weights, values)
            return carry

        lax.fori_loop(0, heads // G, group_step, 0)

    for k in range(nz):
        if k > 0:
            line_copies[k - 1].wait_recv()
            core_copies.append(to_sibling(k))
        if early:
            core_copies[k].wait_recv()
            scores_of(k)
    if not early:
        for copy in core_copies:
            copy.wait_recv()

    def finish_step(i, carry):
        first = i * per_step
        kcols = pl.ds(pl.multiple_of(first // G * HEAD_SIZE, HEAD_SIZE), HEAD_SIZE)
        score_grads = [[] for _ in range(nz)]
        factors, scales = [], []
        for j in range(per_step):
            rows = pl.ds(pl.multiple_of((first + j) * BLK, BLK), BLK)
            cols = pl.ds(pl.multiple_of((first + j) * HEAD_SIZE, HEAD_SIZE), HEAD_SIZE)
            tops = [tops_buf[k, rows, :] for k in range(nz)]
            top = functools.reduce(jnp.maximum, tops)
            factor = [jnp.exp2(t - top) for t in tops]
            attended, total = 0.0, 0.0
            for k in range(nz):
                attended += factor[k] * sums_buf[k, rows, :HEAD_SIZE]
                total += factor[k] * sums_buf[k, rows, HEAD_SIZE:]
            inverse = 1.0 / total
            attended = attended * inverse
            att[:, cols] = attended.astype(BF16)
            inner = jnp.sum(attended * og[:, cols].astype(F32), axis=-1, keepdims=True)
            for k in range(nz):
                weights = weights_buf[k, rows, :].astype(F32)
                score_grads[k].append((weights * (grads_buf[k, rows, :] - inner)).astype(BF16))
            factors.append(factor)
            scales.append(inverse * scaling)
        parts = [
            dot_nn(jnp.concatenate(score_grads[k], axis=0), kv[k, :, kcols]) for k in range(nz)
        ]
        for j in range(per_step):
            cols = pl.ds(pl.multiple_of((first + j) * HEAD_SIZE, HEAD_SIZE), HEAD_SIZE)
            query_grad = 0.0
            for k in range(nz):
                query_grad += factors[j][k] * parts[k][j * BLK : (j + 1) * BLK]
            qg[:, cols] = (query_grad * scales[j]).astype(BF16)
        return carry

    def head_step(i, carry):
        first = i * per_step
        group = first // G
        kcols = pl.ds(pl.multiple_of(group * HEAD_SIZE, HEAD_SIZE), HEAD_SIZE)
        vcols = pl.ds(pl.multiple_of(kvw + group * HEAD_SIZE, HEAD_SIZE), HEAD_SIZE)
        key_rows = kv[:, :, kcols].reshape(keys, HEAD_SIZE)
        value_rows = kv[:, :, vcols].reshape(keys, HEAD_SIZE)
        all_weights, all_grads, all_inverse = [], [], []
        for j in range(per_step):
            h = first + j
            cols = pl.ds(pl.multiple_of(h * HEAD_SIZE, HEAD_SIZE), HEAD_SIZE)
            scores = dot_nt(q[:, cols], key_rows)
            weight_grad = dot_nt(og[:, cols], value_rows)
            scores = scores * (scaling * LOG2E) + bias[pl.ds(h, 1), :]
            weights = jnp.exp2(scores - jnp.max(scores, axis=-1, keepdims=True))
            inverse = 1.0 / jnp.sum(weights, axis=-1, keepdims=True)
            inner = jnp.sum(weights * weight_grad, axis=-1, keepdims=True) * inverse
            all_weights.append(weights.astype(BF16))
            all_grads.append((weights * (weight_grad - inner)).astype(BF16))
            all_inverse.append(inverse)
        attended = dot_nn(jnp.concatenate(all_weights, axis=0), value_rows)
        query_grad = dot_nn(jnp.concatenate(all_grads, axis=0), key_rows)
        for j in range(per_step):
            cols = pl.ds(pl.multiple_of((first + j) * HEAD_SIZE, HEAD_SIZE), HEAD_SIZE)
            rows = slice(j * BLK, (j + 1) * BLK)
            att[:, cols] = (attended[rows] * all_inverse[j]).astype(BF16)
            qg[:, cols] = (query_grad[rows] * (all_inverse[j] * scaling)).astype(BF16)
        return carry

    lax.fori_loop(0, heads // per_step, finish_step if early else head_step, 0)
    att_store = pltpu.make_async_copy(att, att_hbm, store_sem.at[0])
    att_store.start()

    low_grad = (ADAPTER_GAIN * dot_nt(qg[...], up[...])).astype(BF16)

    dpart, upart = wd // parts, wu // parts

    def chunk(chip, part, kind):
        p = lax.rem(dp + chip, ndp) * 2 + kind
        dcols = pl.ds(pl.multiple_of(p * wd + part * dpart, 128), dpart)
        ucols = pl.ds(pl.multiple_of(p * wu + part * upart, 128), upart)
        part_down = dot_tn(low_grad, x[:, dcols])
        part_up = ADAPTER_GAIN * dot_tn(low_rank, qg[:, ucols])
        return jnp.concatenate([part_down, part_up], axis=1)

    order = [(part, chip) for part in range(parts) for chip in list(range(1, ndp)) + [0]]
    pair_copies, rs_copies, gz_copies, ag_copies, af_copies = {}, {}, {}, {}, {}
    for part, chip in order:
        n = part * ndp + chip
        sbuf[n] = chunk(chip, part, 1 - core).astype(BF16)
        pair_copies[n] = send(sbuf.at[n], pbuf.at[n], p_send.at[n], p_recv.at[n], sibling)
    sums = {}
    for part, chip in order:
        n = part * ndp + chip
        own = chunk(chip, part, core)
        pair_copies[n].wait_recv()
        own += pbuf[n].astype(F32)
        if chip == 0:
            sums[part] = own
        else:
            gbuf[n] = own.astype(BF16)
            rs_copies[n] = send(gbuf.at[n], rbuf.at[n], rs_send.at[n], rs_recv.at[n], plane_id(chip))
    for part in range(parts):
        total = sums[part]
        for chip in range(1, ndp):
            n = part * ndp + chip
            rs_copies[n].wait_recv()
            total += rbuf[n].astype(F32)
        slot = part * nz + z
        zbuf[slot] = total.astype(BF16)
        for k in range(1, nz):
            n = part * nz + k
            gz_copies[n] = send(zbuf.at[slot], zbuf.at[slot], gz_send.at[n], gz_recv.at[n], line_id(k))

    def forward(part, chip):
        n = part * ndp + chip
        rows = abuf.at[part * na + lax.rem(dp + ndp - chip, ndp) * 2 + core]
        return send(rows, rows, af_send.at[n], af_recv.at[n], sibling)

    for part in range(parts):
        for k in range(1, nz):
            gz_copies[part * nz + k].wait_recv()
        total = zbuf[part * nz].astype(F32)
        for i in range(1, nz):
            total += zbuf[part * nz + i].astype(F32)
        rows = abuf.at[part * na + dp * 2 + core]
        rows[...] = total.astype(BF16)
        for chip in range(1, ndp):
            n = part * ndp + chip
            ag_copies[n] = send(rows, rows, ag_send.at[n], ag_recv.at[n], plane_id(chip))
        af_copies[part * ndp] = forward(part, 0)
    for part in range(parts):
        for chip in range(1, ndp):
            ag_copies[part * ndp + chip].wait_recv()
            af_copies[part * ndp + chip] = forward(part, chip)
    for copy in line_copies + core_copies:
        copy.wait_send()
    for copies in (pair_copies, rs_copies, gz_copies, ag_copies, af_copies):
        for copy in copies.values():
            copy.wait_send()
    loads[5].wait()
    loads[6].wait()
    for copy in af_copies.values():
        copy.wait_recv()
    norm = (BLK * nctx * ndp) ** (-0.5)
    for p in range(na):
        for part in range(parts):
            total = abuf[part * na + p].astype(F32) * norm
            dfirst, ufirst = p * wd + part * dpart, p * wu + part * upart
            step_down[:, dfirst : dfirst + dpart] += total[:, :dpart]
            step_up[:, ufirst : ufirst + upart] += total[:, dpart:]
    stores = [
        pltpu.make_async_copy(step_down, step_down_hbm, store_sem.at[1]),
        pltpu.make_async_copy(step_up, step_up_hbm, store_sem.at[2]),
    ]
    for copy in stores:
        copy.start()
    for copy in [att_store] + stores:
        copy.wait()


def hand_over(*refs):
    sources, targets, held = refs[:3], refs[3:6], refs[6:9]
    in_sem, out_sem = refs[9:]
    first, second = [], []
    for i in range(3):
        rows = sources[i].shape[0] // 2
        for j in range(2):
            part, n = pl.ds(j * rows, rows), 2 * i + j
            first.append(
                pltpu.make_async_copy(sources[i].at[part], held[i].at[part], in_sem.at[n])
            )
            second.append(
                pltpu.make_async_copy(held[i].at[part], targets[i].at[part], out_sem.at[n])
            )
    for copy in first:
        copy.start()
    for arrive, leave in zip(first, second):
        arrive.wait()
        leave.start()
    for copy in second:
        copy.wait()


def body(
    ndp,
    nctx,
    normed_layer_input,
    frozen_query_rows,
    projected_keys,
    projected_values,
    output_gradient,
    adapter_down,
    adapter_up,
    langevin_down_noise,
    langevin_up_noise,
    listed_key_blocks,
    head_live_slots,
):
    tok, width = normed_layer_input.shape[1:]
    qw, kvw = frozen_query_rows.shape[2], projected_keys.shape[2]
    rank = adapter_up.shape[0]
    heads = qw // HEAD_SIZE
    keys = nctx * tok
    nz, na = nctx // 2, ndp * 2
    parts = 1 if width % (256 * na) or qw % (256 * na) else 2
    piece = (width + qw) // (na * parts)
    early = 2 * heads * tok * keys * 4 <= 2**24
    per_step = 4 if early else 1
    any_spec = pl.BlockSpec(memory_space=pl.ANY)
    vmem_spec = pl.BlockSpec(memory_space=pltpu.VMEM)
    smem_spec = pl.BlockSpec(memory_space=pltpu.SMEM)
    dma = pltpu.SemaphoreType.DMA
    held_rows = (nz, heads * tok) if early else (1, 16)
    results = (
        jax.ShapeDtypeStruct((tok, qw), BF16),
        jax.ShapeDtypeStruct((rank, width), F32),
        jax.ShapeDtypeStruct((rank, qw), F32),
    )
    outputs = pl.pallas_call(
        functools.partial(kernel, ndp, nctx, parts, per_step, early),
        out_shape=results,
        in_specs=[any_spec] * 7 + [vmem_spec] * 3 + [smem_spec],
        out_specs=(any_spec,) * 3,
        scratch_shapes=[
            pltpu.VMEM((tok, width), BF16),
            pltpu.VMEM((tok, qw), BF16),
            pltpu.VMEM((tok, qw), BF16),
            pltpu.VMEM((nz, 2 * BLK, 2 * kvw), BF16),
            pltpu.VMEM((tok, qw), BF16),
            pltpu.VMEM((tok, qw), BF16),
            pltpu.VMEM((tok, qw), BF16),
            pltpu.VMEM((rank, width), F32),
            pltpu.VMEM((rank, qw), F32),
            pltpu.VMEM((heads, keys), F32),
            pltpu.VMEM(held_rows + (2 * BLK,), BF16),
            pltpu.VMEM(held_rows + (2 * BLK,), F32),
            pltpu.VMEM(held_rows + (2 * HEAD_SIZE,), F32),
            pltpu.VMEM(held_rows + (HEAD_SIZE,), F32),
            pltpu.VMEM((parts * ndp, rank, piece), BF16),
            pltpu.VMEM((parts * ndp, rank, piece), BF16),
            pltpu.VMEM((parts * ndp, rank, piece), BF16),
            pltpu.VMEM((parts * ndp, rank, piece), BF16),
            pltpu.VMEM((parts * nz, rank, piece), BF16),
            pltpu.VMEM((parts * na, rank, piece), BF16),
            dma((7,)),
            dma((3,)),
            dma((nz,)),
            dma((nz,)),
            dma((nz,)),
            dma((nz,)),
            dma((parts * ndp,)),
            dma((parts * ndp,)),
            dma((parts * ndp,)),
            dma((parts * ndp,)),
            dma((parts * nz,)),
            dma((parts * nz,)),
            dma((parts * ndp,)),
            dma((parts * ndp,)),
            dma((parts * ndp,)),
            dma((parts * ndp,)),
        ],
        compiler_params=pltpu.CompilerParams(
            collective_id=0,
            has_side_effects=True,
            vmem_limit_bytes=60 * 2**20,
        ),
        name="adapter_attention",
    )(
        normed_layer_input[0],
        frozen_query_rows[0],
        projected_keys[0],
        projected_values[0],
        output_gradient[0],
        langevin_down_noise.T,
        langevin_up_noise,
        adapter_down.T,
        adapter_up,
        listed_key_blocks.transpose(2, 1, 0),
        head_live_slots,
    )
    attended, step_down, step_up = pl.pallas_call(
        hand_over,
        out_shape=results,
        in_specs=[any_spec] * 3,
        out_specs=(any_spec,) * 3,
        scratch_shapes=[pltpu.VMEM(r.shape, r.dtype) for r in results] + [dma((6,)), dma((6,))],
        compiler_params=pltpu.CompilerParams(vmem_limit_bytes=60 * 2**20),
        name="hand_over",
    )(*outputs)
    return attended[None], step_down.T, step_up


def solution(mesh):
    rows = P("dp", "ctx", None)
    return jax.shard_map(
        functools.partial(body, mesh.shape["dp"], mesh.shape["ctx"]),
        mesh=mesh,
        in_specs=(rows,) * 5 + (P(),) * 6,
        out_specs=(rows, P(), P()),
        check_vma=False,
    )
```

```python
import functools

import jax
import jax.numpy as jnp
from jax import lax
from jax.experimental import pallas as pl
from jax.experimental.pallas import tpu as pltpu
from jax.sharding import PartitionSpec as P

HEAD_SIZE = 128
G = 8
BLK = 128
ADAPTER_GAIN = 2.0
MASK_VALUE = -1e30
LOG2E = 1.4426950408889634
MESH = pl.DeviceIdType.MESH
F32 = jnp.float32
BF16 = jnp.bfloat16


def dot_nt(a, b):
    return lax.dot_general(a, b, (((1,), (1,)), ((), ())), preferred_element_type=F32)


def dot_tn(a, b):
    return lax.dot_general(a, b, (((0,), (0,)), ((), ())), preferred_element_type=F32)


def dot_nn(a, b):
    return jnp.dot(a, b, preferred_element_type=F32)


def send(source, target, send_sem, recv_sem, device):
    copy = pltpu.make_async_remote_copy(
        src_ref=source,
        dst_ref=target,
        send_sem=send_sem,
        recv_sem=recv_sem,
        device_id=device,
        device_id_type=MESH,
    )
    copy.start()
    return copy


def kernel(
    ndp,
    nctx,
    parts,
    per_step,
    early,
    x_hbm,
    frozen_hbm,
    k_hbm,
    v_hbm,
    og_hbm,
    noise_down_hbm,
    noise_up_hbm,
    down_t,
    up,
    lists,
    live,
    att_hbm,
    step_down_hbm,
    step_up_hbm,
    x,
    frozen,
    og,
    kv,
    q,
    qg,
    att,
    step_down,
    step_up,
    bias,
    weights_buf,
    grads_buf,
    sums_buf,
    tops_buf,
    gown,
    sbuf,
    pbuf,
    gbuf,
    rbuf,
    zbuf,
    abuf,
    load_sem,
    store_sem,
    z_send,
    z_recv,
    c_send,
    c_recv,
    p_send,
    p_recv,
    rs_send,
    rs_recv,
    gz_send,
    gz_recv,
    ag_send,
    ag_recv,
    af_send,
    af_recv,
):
    dp, ctx = lax.axis_index("dp"), lax.axis_index("ctx")
    nz, na = nctx // 2, ndp * 2
    z, core = lax.div(ctx, 2), lax.rem(ctx, 2)
    kvw = k_hbm.shape[1]
    width = x.shape[1]
    qw = q.shape[1]
    heads = qw // HEAD_SIZE
    wd, wu = width // na, qw // na
    keys = nctx * BLK

    own_rows = pl.ds(pl.multiple_of(core * BLK, BLK), BLK)

    def line(k):
        if nz & (nz - 1):
            return lax.rem(z + nz - k, nz)
        other, bit = z, 1
        while bit < nz:
            if k & bit:
                other = other + bit * (1 - 2 * lax.rem(lax.div(z, bit), 2))
            bit *= 2
        return other

    sibling = (dp, z * 2 + 1 - core)

    def plane_id(k):
        return (lax.rem(dp + k, ndp), ctx)

    def line_id(k):
        to = lax.rem(z + k, nz) if nz & (nz - 1) else line(k)
        return (dp, to * 2 + core)

    loads = []
    for i, (src, dst) in enumerate(
        (
            (k_hbm, kv.at[0, own_rows, pl.ds(0, kvw)]),
            (v_hbm, kv.at[0, own_rows, pl.ds(kvw, kvw)]),
            (x_hbm, x),
            (frozen_hbm, frozen),
            (og_hbm, og),
            (noise_down_hbm, step_down),
            (noise_up_hbm, step_up),
        )
    ):
        copy = pltpu.make_async_copy(src, dst, load_sem.at[i])
        copy.start()
        loads.append(copy)

    barrier = pltpu.get_barrier_semaphore()
    partners = [sibling]
    partners += [plane_id(k) for k in range(1, ndp)]
    partners += [line_id(k) for k in range(1, nz)]
    for partner in partners:
        pl.semaphore_signal(barrier, inc=1, device_id=partner, device_id_type=MESH)

    slots, nqb = lists.shape[:2]
    mine = lax.broadcasted_iota(jnp.int32, lists.shape, 1) == ctx
    local = jnp.sum(jnp.where(mine, lists[...].astype(F32), 0.0), axis=1)
    head_iota = lax.broadcasted_iota(jnp.int32, (1, heads), 1)
    live_row = jnp.zeros((1, heads), jnp.int32)
    for h in range(heads):
        live_row = jnp.where(head_iota == h, live[h], live_row)
    block_iota = lax.broadcasted_iota(jnp.int32, (nqb, heads), 0).astype(F32)
    count = jnp.zeros((nqb, heads), F32)
    for j in range(slots):
        listed = jnp.where(live_row > j, local[j : j + 1, :], -1.0)
        count += jnp.where(block_iota == listed, 1.0, 0.0)
    lane = lax.broadcasted_iota(jnp.int32, (1, keys), 1)
    held = jnp.zeros((1, keys), jnp.int32)
    for k in range(nz):
        held = jnp.where(lane // (2 * BLK) == k, line(k) * 2, held)
    held += (lane // BLK) % 2
    spread = jnp.where(lax.broadcasted_iota(jnp.int32, (nqb, keys), 0) == held, 1.0, 0.0)
    count = dot_tn(count, spread)
    bias[...] = jnp.where(count > 0.5, jnp.log(jnp.maximum(count, 1.0)) * LOG2E, MASK_VALUE)

    pl.semaphore_wait(barrier, len(partners))

    loads[0].wait()
    loads[1].wait()
    line_copies = []
    for k in range(1, nz):
        source, target = kv.at[0, own_rows, :], kv.at[k, own_rows, :]
        line_copies.append(send(source, target, z_send.at[k], z_recv.at[k], line_id(k)))

    def to_sibling(k):
        rows = kv.at[k, own_rows, :]
        return send(rows, rows, c_send.at[k], c_recv.at[k], sibling)

    core_copies = [to_sibling(0)]

    loads[2].wait()
    low_rank = dot_nt(x[...], down_t[...]).astype(BF16)
    tok_iota = [lax.broadcasted_iota(jnp.int32, (BLK, BLK), i) for i in range(2)]
    identity = jnp.where(tok_iota[0] == tok_iota[1], 1.0, 0.0).astype(BF16)
    low_rank_t = dot_tn(low_rank, identity).astype(BF16)
    loads[3].wait()
    q[...] = (frozen[...].astype(F32) + ADAPTER_GAIN * dot_nn(low_rank, up[...])).astype(BF16)

    loads[4].wait()
    scaling = HEAD_SIZE ** (-0.5)
    pair = 2 * BLK

    def stacked(ref, first, number):
        return jnp.concatenate(
            [
                ref[:, pl.ds(pl.multiple_of((first + j) * HEAD_SIZE, HEAD_SIZE), HEAD_SIZE)]
                for j in range(number)
            ],
            axis=0,
        )

    def scores_of(k):
        def group_step(group, carry):
            kcols = pl.ds(pl.multiple_of(group * HEAD_SIZE, HEAD_SIZE), HEAD_SIZE)
            vcols = pl.ds(pl.multiple_of(kvw + group * HEAD_SIZE, HEAD_SIZE), HEAD_SIZE)
            rows = pl.ds(pl.multiple_of(group * G * BLK, G * BLK), G * BLK)
            scores = dot_nt(stacked(q, group * G, G), kv[k, :, kcols])
            grads_buf[k, rows, :] = dot_nt(stacked(og, group * G, G), kv[k, :, vcols])
            group_bias = bias[pl.ds(pl.multiple_of(group * G, G), G), k * pair : (k + 1) * pair]
            all_weights = []
            for j in range(G):
                head_rows = pl.ds(pl.multiple_of((group * G + j) * BLK, BLK), BLK)
                head_scores = scores[j * BLK : (j + 1) * BLK] * (scaling * LOG2E)
                head_scores += group_bias[j : j + 1]
                top = jnp.max(head_scores, axis=-1, keepdims=True)
                tops_buf[k, head_rows, :] = jnp.broadcast_to(top, (BLK, HEAD_SIZE))
                all_weights.append(jnp.exp2(head_scores - top).astype(BF16))
            weights = jnp.concatenate(all_weights, axis=0)
            weights_buf[k, rows, :] = weights
            values = jnp.concatenate([kv[k, :, vcols], jnp.ones((pair, HEAD_SIZE), BF16)], axis=1)
            sums_buf[k, rows, :] = dot_nn(weights, values)
            return carry

        lax.fori_loop(0, heads // G, group_step, 0)

    for k in range(nz):
        if k > 0:
            line_copies[k - 1].wait_recv()
            core_copies.append(to_sibling(k))
        if early:
            core_copies[k].wait_recv()
            scores_of(k)
    if not early:
        for copy in core_copies:
            copy.wait_recv()

    def finish_step(i, carry):
        first = i * per_step
        kcols = pl.ds(pl.multiple_of(first // G * HEAD_SIZE, HEAD_SIZE), HEAD_SIZE)
        score_grads = [[] for _ in range(nz)]
        factors, scales = [], []
        for j in range(per_step):
            rows = pl.ds(pl.multiple_of((first + j) * BLK, BLK), BLK)
            cols = pl.ds(pl.multiple_of((first + j) * HEAD_SIZE, HEAD_SIZE), HEAD_SIZE)
            tops = [tops_buf[k, rows, :] for k in range(nz)]
            top = functools.reduce(jnp.maximum, tops)
            factor = [jnp.exp2(t - top) for t in tops]
            attended, total = 0.0, 0.0
            for k in range(nz):
                attended += factor[k] * sums_buf[k, rows, :HEAD_SIZE]
                total += factor[k] * sums_buf[k, rows, HEAD_SIZE:]
            inverse = 1.0 / total
            attended = attended * inverse
            att[:, cols] = attended.astype(BF16)
            inner = jnp.sum(attended * og[:, cols].astype(F32), axis=-1, keepdims=True)
            for k in range(nz):
                weights = weights_buf[k, rows, :].astype(F32)
                score_grads[k].append((weights * (grads_buf[k, rows, :] - inner)).astype(BF16))
            factors.append(factor)
            scales.append(inverse * scaling)
        parts = [
            dot_nn(jnp.concatenate(score_grads[k], axis=0), kv[k, :, kcols]) for k in range(nz)
        ]
        for j in range(per_step):
            cols = pl.ds(pl.multiple_of((first + j) * HEAD_SIZE, HEAD_SIZE), HEAD_SIZE)
            query_grad = 0.0
            for k in range(nz):
                query_grad += factors[j][k] * parts[k][j * BLK : (j + 1) * BLK]
            qg[:, cols] = (query_grad * scales[j]).astype(BF16)
        return carry

    def head_step(i, carry):
        first = i * per_step
        group = first // G
        kcols = pl.ds(pl.multiple_of(group * HEAD_SIZE, HEAD_SIZE), HEAD_SIZE)
        vcols = pl.ds(pl.multiple_of(kvw + group * HEAD_SIZE, HEAD_SIZE), HEAD_SIZE)
        key_rows = kv[:, :, kcols].reshape(keys, HEAD_SIZE)
        value_rows = kv[:, :, vcols].reshape(keys, HEAD_SIZE)
        all_weights, all_grads, all_inverse = [], [], []
        for j in range(per_step):
            h = first + j
            cols = pl.ds(pl.multiple_of(h * HEAD_SIZE, HEAD_SIZE), HEAD_SIZE)
            scores = dot_nt(q[:, cols], key_rows)
            weight_grad = dot_nt(og[:, cols], value_rows)
            scores = scores * (scaling * LOG2E) + bias[pl.ds(h, 1), :]
            weights = jnp.exp2(scores - jnp.max(scores, axis=-1, keepdims=True))
            inverse = 1.0 / jnp.sum(weights, axis=-1, keepdims=True)
            inner = jnp.sum(weights * weight_grad, axis=-1, keepdims=True) * inverse
            all_weights.append(weights.astype(BF16))
            all_grads.append((weights * (weight_grad - inner)).astype(BF16))
            all_inverse.append(inverse)
        attended = dot_nn(jnp.concatenate(all_weights, axis=0), value_rows)
        query_grad = dot_nn(jnp.concatenate(all_grads, axis=0), key_rows)
        for j in range(per_step):
            cols = pl.ds(pl.multiple_of((first + j) * HEAD_SIZE, HEAD_SIZE), HEAD_SIZE)
            rows = slice(j * BLK, (j + 1) * BLK)
            att[:, cols] = (attended[rows] * all_inverse[j]).astype(BF16)
            qg[:, cols] = (query_grad[rows] * (all_inverse[j] * scaling)).astype(BF16)
        return carry

    lax.fori_loop(0, heads // per_step, finish_step if early else head_step, 0)
    att_store = pltpu.make_async_copy(att, att_hbm, store_sem.at[0])
    att_store.start()

    low_grad_t = (ADAPTER_GAIN * dot_nt(up[...], qg[...])).astype(BF16)

    dpart, upart = wd // parts, wu // parts

    def owner(chip, kind):
        return lax.rem(dp + chip, ndp) * 2 + kind

    order = [(part, chip) for part in range(parts) for chip in list(range(1, ndp)) + [0]]
    pair_copies, rs_copies, gz_copies, ag_copies, af_copies = {}, {}, {}, {}, {}
    for part in range(parts):
        for p in range(na):
            dfirst, ufirst = p * wd + part * dpart, p * wu + part * upart
            part_down = dot_nn(low_grad_t, x[:, dfirst : dfirst + dpart])
            part_up = ADAPTER_GAIN * dot_nn(low_rank_t, qg[:, ufirst : ufirst + upart])
            both = jnp.concatenate([part_down, part_up], axis=1)
            gown[part * na + p] = both
            sbuf[part * na + p] = both.astype(BF16)
        for chip in list(range(1, ndp)) + [0]:
            n = part * ndp + chip
            source = sbuf.at[part * na + owner(chip, 1 - core)]
            pair_copies[n] = send(source, pbuf.at[n], p_send.at[n], p_recv.at[n], sibling)
    sums = {}
    for part, chip in order:
        n = part * ndp + chip
        own = gown[part * na + owner(chip, core)]
        pair_copies[n].wait_recv()
        own += pbuf[n].astype(F32)
        if chip == 0:
            sums[part] = own
        else:
            gbuf[n] = own.astype(BF16)
            rs_copies[n] = send(gbuf.at[n], rbuf.at[n], rs_send.at[n], rs_recv.at[n], plane_id(chip))
    for part in range(parts):
        total = sums[part]
        for chip in range(1, ndp):
            n = part * ndp + chip
            rs_copies[n].wait_recv()
            total += rbuf[n].astype(F32)
        slot = part * nz + z
        zbuf[slot] = total.astype(BF16)
        for k in range(1, nz):
            n = part * nz + k
            gz_copies[n] = send(zbuf.at[slot], zbuf.at[slot], gz_send.at[n], gz_recv.at[n], line_id(k))

    def forward(part, chip):
        n = part * ndp + chip
        rows = abuf.at[part * na + lax.rem(dp + ndp - chip, ndp) * 2 + core]
        return send(rows, rows, af_send.at[n], af_recv.at[n], sibling)

    for part in range(parts):
        for k in range(1, nz):
            gz_copies[part * nz + k].wait_recv()
        total = zbuf[part * nz].astype(F32)
        for i in range(1, nz):
            total += zbuf[part * nz + i].astype(F32)
        rows = abuf.at[part * na + dp * 2 + core]
        rows[...] = total.astype(BF16)
        for chip in range(1, ndp):
            n = part * ndp + chip
            ag_copies[n] = send(rows, rows, ag_send.at[n], ag_recv.at[n], plane_id(chip))
        af_copies[part * ndp] = forward(part, 0)
    for part in range(parts):
        for chip in range(1, ndp):
            ag_copies[part * ndp + chip].wait_recv()
            af_copies[part * ndp + chip] = forward(part, chip)
    for copy in line_copies + core_copies:
        copy.wait_send()
    for copies in (pair_copies, rs_copies, gz_copies, ag_copies, af_copies):
        for copy in copies.values():
            copy.wait_send()
    loads[5].wait()
    loads[6].wait()
    for copy in af_copies.values():
        copy.wait_recv()
    norm = (BLK * nctx * ndp) ** (-0.5)
    for p in range(na):
        for part in range(parts):
            total = abuf[part * na + p].astype(F32) * norm
            dfirst, ufirst = p * wd + part * dpart, p * wu + part * upart
            step_down[:, dfirst : dfirst + dpart] += total[:, :dpart]
            step_up[:, ufirst : ufirst + upart] += total[:, dpart:]
    stores = [
        pltpu.make_async_copy(step_down, step_down_hbm, store_sem.at[1]),
        pltpu.make_async_copy(step_up, step_up_hbm, store_sem.at[2]),
    ]
    for copy in stores:
        copy.start()
    for copy in [att_store] + stores:
        copy.wait()


def hand_over(*refs):
    sources, targets, held = refs[:3], refs[3:6], refs[6:9]
    in_sem, out_sem = refs[9:]
    first, second = [], []
    for i in range(3):
        rows = sources[i].shape[0] // 2
        for j in range(2):
            part, n = pl.ds(j * rows, rows), 2 * i + j
            first.append(
                pltpu.make_async_copy(sources[i].at[part], held[i].at[part], in_sem.at[n])
            )
            second.append(
                pltpu.make_async_copy(held[i].at[part], targets[i].at[part], out_sem.at[n])
            )
    for copy in first:
        copy.start()
    for arrive, leave in zip(first, second):
        arrive.wait()
        leave.start()
    for copy in second:
        copy.wait()


def body(
    ndp,
    nctx,
    normed_layer_input,
    frozen_query_rows,
    projected_keys,
    projected_values,
    output_gradient,
    adapter_down,
    adapter_up,
    langevin_down_noise,
    langevin_up_noise,
    listed_key_blocks,
    head_live_slots,
):
    tok, width = normed_layer_input.shape[1:]
    qw, kvw = frozen_query_rows.shape[2], projected_keys.shape[2]
    rank = adapter_up.shape[0]
    heads = qw // HEAD_SIZE
    keys = nctx * tok
    nz, na = nctx // 2, ndp * 2
    parts = 1 if width % (256 * na) or qw % (256 * na) else 2
    piece = (width + qw) // (na * parts)
    early = 2 * heads * tok * keys * 4 <= 2**24
    per_step = 4 if early else 1
    any_spec = pl.BlockSpec(memory_space=pl.ANY)
    vmem_spec = pl.BlockSpec(memory_space=pltpu.VMEM)
    smem_spec = pl.BlockSpec(memory_space=pltpu.SMEM)
    dma = pltpu.SemaphoreType.DMA
    held_rows = (nz, heads * tok) if early else (1, 16)
    results = (
        jax.ShapeDtypeStruct((tok, qw), BF16),
        jax.ShapeDtypeStruct((rank, width), F32),
        jax.ShapeDtypeStruct((rank, qw), F32),
    )
    outputs = pl.pallas_call(
        functools.partial(kernel, ndp, nctx, parts, per_step, early),
        out_shape=results,
        in_specs=[any_spec] * 7 + [vmem_spec] * 3 + [smem_spec],
        out_specs=(any_spec,) * 3,
        scratch_shapes=[
            pltpu.VMEM((tok, width), BF16),
            pltpu.VMEM((tok, qw), BF16),
            pltpu.VMEM((tok, qw), BF16),
            pltpu.VMEM((nz, 2 * BLK, 2 * kvw), BF16),
            pltpu.VMEM((tok, qw), BF16),
            pltpu.VMEM((tok, qw), BF16),
            pltpu.VMEM((tok, qw), BF16),
            pltpu.VMEM((rank, width), F32),
            pltpu.VMEM((rank, qw), F32),
            pltpu.VMEM((heads, keys), F32),
            pltpu.VMEM(held_rows + (2 * BLK,), BF16),
            pltpu.VMEM(held_rows + (2 * BLK,), F32),
            pltpu.VMEM(held_rows + (2 * HEAD_SIZE,), F32),
            pltpu.VMEM(held_rows + (HEAD_SIZE,), F32),
            pltpu.VMEM((parts * na, rank, piece), F32),
            pltpu.VMEM((parts * na, rank, piece), BF16),
            pltpu.VMEM((parts * ndp, rank, piece), BF16),
            pltpu.VMEM((parts * ndp, rank, piece), BF16),
            pltpu.VMEM((parts * ndp, rank, piece), BF16),
            pltpu.VMEM((parts * nz, rank, piece), BF16),
            pltpu.VMEM((parts * na, rank, piece), BF16),
            dma((7,)),
            dma((3,)),
            dma((nz,)),
            dma((nz,)),
            dma((nz,)),
            dma((nz,)),
            dma((parts * ndp,)),
            dma((parts * ndp,)),
            dma((parts * ndp,)),
            dma((parts * ndp,)),
            dma((parts * nz,)),
            dma((parts * nz,)),
            dma((parts * ndp,)),
            dma((parts * ndp,)),
            dma((parts * ndp,)),
            dma((parts * ndp,)),
        ],
        compiler_params=pltpu.CompilerParams(
            collective_id=0,
            has_side_effects=True,
            vmem_limit_bytes=60 * 2**20,
        ),
        name="adapter_attention",
    )(
        normed_layer_input[0],
        frozen_query_rows[0],
        projected_keys[0],
        projected_values[0],
        output_gradient[0],
        langevin_down_noise.T,
        langevin_up_noise,
        adapter_down.T,
        adapter_up,
        listed_key_blocks.transpose(2, 1, 0),
        head_live_slots,
    )
    attended, step_down, step_up = pl.pallas_call(
        hand_over,
        out_shape=results,
        in_specs=[any_spec] * 3,
        out_specs=(any_spec,) * 3,
        scratch_shapes=[pltpu.VMEM(r.shape, r.dtype) for r in results] + [dma((6,)), dma((6,))],
        compiler_params=pltpu.CompilerParams(vmem_limit_bytes=60 * 2**20),
        name="hand_over",
    )(*outputs)
    return attended[None], step_down.T, step_up


def solution(mesh):
    rows = P("dp", "ctx", None)
    return jax.shard_map(
        functools.partial(body, mesh.shape["dp"], mesh.shape["ctx"]),
        mesh=mesh,
        in_specs=(rows,) * 5 + (P(),) * 6,
        out_specs=(rows, P(), P()),
        check_vma=False,
    )
```

```python
import functools

import jax
import jax.numpy as jnp
from jax import lax
from jax.experimental import pallas as pl
from jax.experimental.pallas import tpu as pltpu
from jax.sharding import PartitionSpec as P

HEAD_SIZE = 128
G = 8
BLK = 128
ADAPTER_GAIN = 2.0
MASK_VALUE = -1e30
LOG2E = 1.4426950408889634
MESH = pl.DeviceIdType.MESH
F32 = jnp.float32
BF16 = jnp.bfloat16


def dot_nt(a, b):
    return lax.dot_general(a, b, (((1,), (1,)), ((), ())), preferred_element_type=F32)


def dot_tn(a, b):
    return lax.dot_general(a, b, (((0,), (0,)), ((), ())), preferred_element_type=F32)


def dot_nn(a, b):
    return jnp.dot(a, b, preferred_element_type=F32)


def remote(source, target, send_sem, recv_sem, device):
    return pltpu.make_async_remote_copy(
        src_ref=source,
        dst_ref=target,
        send_sem=send_sem,
        recv_sem=recv_sem,
        device_id=device,
        device_id_type=MESH,
    )


def send(*ends):
    copy = remote(*ends)
    copy.start()
    return copy


def kernel(
    ndp,
    nctx,
    parts,
    per_step,
    early,
    x_hbm,
    frozen_hbm,
    k_hbm,
    v_hbm,
    og_hbm,
    noise_down_hbm,
    noise_up_hbm,
    down_t,
    up,
    lists,
    live,
    att_hbm,
    step_down_hbm,
    step_up_hbm,
    x,
    frozen,
    og,
    kv,
    q,
    qg,
    att,
    step_down,
    step_up,
    bias,
    weights_buf,
    grads_buf,
    sums_buf,
    tops_buf,
    gown,
    sbuf,
    pbuf,
    gbuf,
    rbuf,
    zbuf,
    abuf,
    load_sem,
    store_sem,
    z_send,
    z_recv,
    c_send,
    c_recv,
    p_send,
    p_recv,
    rs_send,
    rs_recv,
    gz_send,
    gz_recv,
    ag_send,
    ag_recv,
    af_send,
    af_recv,
):
    dp, ctx = lax.axis_index("dp"), lax.axis_index("ctx")
    nz, na = nctx // 2, ndp * 2
    z, core = lax.div(ctx, 2), lax.rem(ctx, 2)
    kvw = k_hbm.shape[1]
    width = x.shape[1]
    qw = q.shape[1]
    heads = qw // HEAD_SIZE
    wd, wu = width // na, qw // na
    keys = nctx * BLK

    own_rows = pl.ds(pl.multiple_of(core * BLK, BLK), BLK)

    def line(k):
        if nz & (nz - 1):
            return lax.rem(z + nz - k, nz)
        other, bit = z, 1
        while bit < nz:
            if k & bit:
                other = other + bit * (1 - 2 * lax.rem(lax.div(z, bit), 2))
            bit *= 2
        return other

    sibling = (dp, z * 2 + 1 - core)

    def plane_id(k):
        return (lax.rem(dp + k, ndp), ctx)

    def line_id(k):
        to = lax.rem(z + k, nz) if nz & (nz - 1) else line(k)
        return (dp, to * 2 + core)

    loads = []
    for i, (src, dst) in enumerate(
        (
            (k_hbm, kv.at[0, own_rows, pl.ds(0, kvw)]),
            (v_hbm, kv.at[0, own_rows, pl.ds(kvw, kvw)]),
            (x_hbm, x),
            (frozen_hbm, frozen),
            (og_hbm, og),
            (noise_down_hbm, step_down),
            (noise_up_hbm, step_up),
        )
    ):
        copy = pltpu.make_async_copy(src, dst, load_sem.at[i])
        copy.start()
        loads.append(copy)

    barrier = pltpu.get_barrier_semaphore()
    partners = [sibling]
    partners += [plane_id(k) for k in range(1, ndp)]
    partners += [line_id(k) for k in range(1, nz)]
    for partner in partners:
        pl.semaphore_signal(barrier, inc=1, device_id=partner, device_id_type=MESH)

    slots, nqb = lists.shape[:2]
    mine = lax.broadcasted_iota(jnp.int32, lists.shape, 1) == ctx
    local = jnp.sum(jnp.where(mine, lists[...].astype(F32), 0.0), axis=1)
    head_iota = lax.broadcasted_iota(jnp.int32, (1, heads), 1)
    live_row = jnp.zeros((1, heads), jnp.int32)
    for h in range(heads):
        live_row = jnp.where(head_iota == h, live[h], live_row)
    block_iota = lax.broadcasted_iota(jnp.int32, (nqb, heads), 0).astype(F32)
    count = jnp.zeros((nqb, heads), F32)
    for j in range(slots):
        listed = jnp.where(live_row > j, local[j : j + 1, :], -1.0)
        count += jnp.where(block_iota == listed, 1.0, 0.0)
    lane = lax.broadcasted_iota(jnp.int32, (1, keys), 1)
    held = jnp.zeros((1, keys), jnp.int32)
    for k in range(nz):
        held = jnp.where(lane // (2 * BLK) == k, line(k) * 2, held)
    held += (lane // BLK) % 2
    spread = jnp.where(lax.broadcasted_iota(jnp.int32, (nqb, keys), 0) == held, 1.0, 0.0)
    count = dot_tn(count, spread)
    bias[...] = jnp.where(count > 0.5, jnp.log(jnp.maximum(count, 1.0)) * LOG2E, MASK_VALUE)

    pl.semaphore_wait(barrier, len(partners))

    loads[0].wait()
    loads[1].wait()
    line_copies = []
    for k in range(1, nz):
        source, target = kv.at[0, own_rows, :], kv.at[k, own_rows, :]
        line_copies.append(
            remote(source, target, z_send.at[k], z_recv.at[k], line_id(k))
        )
    staged = nz == 4
    middle = (z == 1) | (z == 2)
    line_copies[0].start()
    if staged:
        pl.when(middle)(line_copies[2].start)
    else:
        for copy in line_copies[1:]:
            copy.start()

    def to_sibling(k):
        rows = kv.at[k, own_rows, :]
        return send(rows, rows, c_send.at[k], c_recv.at[k], sibling)

    core_copies = [to_sibling(0)]

    loads[2].wait()
    low_rank = dot_nt(x[...], down_t[...]).astype(BF16)
    if staged:
        line_copies[1].start()
    tok_iota = [lax.broadcasted_iota(jnp.int32, (BLK, BLK), i) for i in range(2)]
    identity = jnp.where(tok_iota[0] == tok_iota[1], 1.0, 0.0).astype(BF16)
    low_rank_t = dot_tn(low_rank, identity).astype(BF16)
    loads[3].wait()
    q[...] = (frozen[...].astype(F32) + ADAPTER_GAIN * dot_nn(low_rank, up[...])).astype(BF16)

    loads[4].wait()
    scaling = HEAD_SIZE ** (-0.5)
    pair = 2 * BLK

    def stacked(ref, first, number):
        return jnp.concatenate(
            [
                ref[:, pl.ds(pl.multiple_of((first + j) * HEAD_SIZE, HEAD_SIZE), HEAD_SIZE)]
                for j in range(number)
            ],
            axis=0,
        )

    def scores_of(k):
        def group_step(group, carry):
            kcols = pl.ds(pl.multiple_of(group * HEAD_SIZE, HEAD_SIZE), HEAD_SIZE)
            vcols = pl.ds(pl.multiple_of(kvw + group * HEAD_SIZE, HEAD_SIZE), HEAD_SIZE)
            rows = pl.ds(pl.multiple_of(group * G * BLK, G * BLK), G * BLK)
            scores = dot_nt(stacked(q, group * G, G), kv[k, :, kcols])
            grads_buf[k, rows, :] = dot_nt(stacked(og, group * G, G), kv[k, :, vcols])
            group_bias = bias[pl.ds(pl.multiple_of(group * G, G), G), k * pair : (k + 1) * pair]
            all_weights = []
            for j in range(G):
                head_rows = pl.ds(pl.multiple_of((group * G + j) * BLK, BLK), BLK)
                head_scores = scores[j * BLK : (j + 1) * BLK] * (scaling * LOG2E)
                head_scores += group_bias[j : j + 1]
                top = jnp.max(head_scores, axis=-1, keepdims=True)
                tops_buf[k, head_rows, :] = jnp.broadcast_to(top, (BLK, HEAD_SIZE))
                all_weights.append(jnp.exp2(head_scores - top).astype(BF16))
            weights = jnp.concatenate(all_weights, axis=0)
            weights_buf[k, rows, :] = weights
            values = jnp.concatenate([kv[k, :, vcols], jnp.ones((pair, HEAD_SIZE), BF16)], axis=1)
            sums_buf[k, rows, :] = dot_nn(weights, values)
            return carry

        lax.fori_loop(0, heads // G, group_step, 0)

    for k in range(nz):
        if k > 0:
            line_copies[k - 1].wait_recv()
            core_copies.append(to_sibling(k))
        if early:
            core_copies[k].wait_recv()
            scores_of(k)
        if staged and k == 0:
            pl.when(jnp.logical_not(middle))(line_copies[2].start)
    if not early:
        for copy in core_copies:
            copy.wait_recv()

    def finish_step(i, carry):
        first = i * per_step
        kcols = pl.ds(pl.multiple_of(first // G * HEAD_SIZE, HEAD_SIZE), HEAD_SIZE)
        score_grads = [[] for _ in range(nz)]
        factors, scales = [], []
        for j in range(per_step):
            rows = pl.ds(pl.multiple_of((first + j) * BLK, BLK), BLK)
            cols = pl.ds(pl.multiple_of((first + j) * HEAD_SIZE, HEAD_SIZE), HEAD_SIZE)
            tops = [tops_buf[k, rows, :] for k in range(nz)]
            top = functools.reduce(jnp.maximum, tops)
            factor = [jnp.exp2(t - top) for t in tops]
            attended, total = 0.0, 0.0
            for k in range(nz):
                attended += factor[k] * sums_buf[k, rows, :HEAD_SIZE]
                total += factor[k] * sums_buf[k, rows, HEAD_SIZE:]
            inverse = 1.0 / total
            attended = attended * inverse
            att[:, cols] = attended.astype(BF16)
            inner = jnp.sum(attended * og[:, cols].astype(F32), axis=-1, keepdims=True)
            for k in range(nz):
                weights = weights_buf[k, rows, :].astype(F32)
                score_grads[k].append((weights * (grads_buf[k, rows, :] - inner)).astype(BF16))
            factors.append(factor)
            scales.append(inverse * scaling)
        parts = [
            dot_nn(jnp.concatenate(score_grads[k], axis=0), kv[k, :, kcols]) for k in range(nz)
        ]
        for j in range(per_step):
            cols = pl.ds(pl.multiple_of((first + j) * HEAD_SIZE, HEAD_SIZE), HEAD_SIZE)
            query_grad = 0.0
            for k in range(nz):
                query_grad += factors[j][k] * parts[k][j * BLK : (j + 1) * BLK]
            qg[:, cols] = (query_grad * scales[j]).astype(BF16)
        return carry

    def head_step(i, carry):
        first = i * per_step
        group = first // G
        kcols = pl.ds(pl.multiple_of(group * HEAD_SIZE, HEAD_SIZE), HEAD_SIZE)
        vcols = pl.ds(pl.multiple_of(kvw + group * HEAD_SIZE, HEAD_SIZE), HEAD_SIZE)
        key_rows = kv[:, :, kcols].reshape(keys, HEAD_SIZE)
        value_rows = kv[:, :, vcols].reshape(keys, HEAD_SIZE)
        all_weights, all_grads, all_inverse = [], [], []
        for j in range(per_step):
            h = first + j
            cols = pl.ds(pl.multiple_of(h * HEAD_SIZE, HEAD_SIZE), HEAD_SIZE)
            scores = dot_nt(q[:, cols], key_rows)
            weight_grad = dot_nt(og[:, cols], value_rows)
            scores = scores * (scaling * LOG2E) + bias[pl.ds(h, 1), :]
            weights = jnp.exp2(scores - jnp.max(scores, axis=-1, keepdims=True))
            inverse = 1.0 / jnp.sum(weights, axis=-1, keepdims=True)
            inner = jnp.sum(weights * weight_grad, axis=-1, keepdims=True) * inverse
            all_weights.append(weights.astype(BF16))
            all_grads.append((weights * (weight_grad - inner)).astype(BF16))
            all_inverse.append(inverse)
        attended = dot_nn(jnp.concatenate(all_weights, axis=0), value_rows)
        query_grad = dot_nn(jnp.concatenate(all_grads, axis=0), key_rows)
        for j in range(per_step):
            cols = pl.ds(pl.multiple_of((first + j) * HEAD_SIZE, HEAD_SIZE), HEAD_SIZE)
            rows = slice(j * BLK, (j + 1) * BLK)
            att[:, cols] = (attended[rows] * all_inverse[j]).astype(BF16)
            qg[:, cols] = (query_grad[rows] * (all_inverse[j] * scaling)).astype(BF16)
        return carry

    lax.fori_loop(0, heads // per_step, finish_step if early else head_step, 0)
    att_store = pltpu.make_async_copy(att, att_hbm, store_sem.at[0])
    att_store.start()

    low_grad_t = (ADAPTER_GAIN * dot_nt(up[...], qg[...])).astype(BF16)

    dpart, upart = wd // parts, wu // parts

    def owner(chip, kind):
        return lax.rem(dp + chip, ndp) * 2 + kind

    order = [(part, chip) for part in range(parts) for chip in list(range(1, ndp)) + [0]]
    pair_copies, rs_copies, gz_copies, ag_copies, af_copies = {}, {}, {}, {}, {}
    for part in range(parts):
        for p in range(na):
            dfirst, ufirst = p * wd + part * dpart, p * wu + part * upart
            part_down = dot_nn(low_grad_t, x[:, dfirst : dfirst + dpart])
            part_up = ADAPTER_GAIN * dot_nn(low_rank_t, qg[:, ufirst : ufirst + upart])
            both = jnp.concatenate([part_down, part_up], axis=1)
            gown[part * na + p] = both
            sbuf[part * na + p] = both.astype(BF16)
        for chip in list(range(1, ndp)) + [0]:
            n = part * ndp + chip
            source = sbuf.at[part * na + owner(chip, 1 - core)]
            pair_copies[n] = send(source, pbuf.at[n], p_send.at[n], p_recv.at[n], sibling)
    sums = {}
    for part, chip in order:
        n = part * ndp + chip
        own = gown[part * na + owner(chip, core)]
        pair_copies[n].wait_recv()
        own += pbuf[n].astype(F32)
        if chip == 0:
            sums[part] = own
        else:
            gbuf[n] = own.astype(BF16)
            rs_copies[n] = send(gbuf.at[n], rbuf.at[n], rs_send.at[n], rs_recv.at[n], plane_id(chip))
    for part in range(parts):
        total = sums[part]
        for chip in range(1, ndp):
            n = part * ndp + chip
            rs_copies[n].wait_recv()
            total += rbuf[n].astype(F32)
        slot = part * nz + z
        zbuf[slot] = total.astype(BF16)
        for k in range(1, nz):
            n = part * nz + k
            gz_copies[n] = send(zbuf.at[slot], zbuf.at[slot], gz_send.at[n], gz_recv.at[n], line_id(k))

    def forward(part, chip):
        n = part * ndp + chip
        rows = abuf.at[part * na + lax.rem(dp + ndp - chip, ndp) * 2 + core]
        return send(rows, rows, af_send.at[n], af_recv.at[n], sibling)

    for part in range(parts):
        for k in range(1, nz):
            gz_copies[part * nz + k].wait_recv()
        total = zbuf[part * nz].astype(F32)
        for i in range(1, nz):
            total += zbuf[part * nz + i].astype(F32)
        rows = abuf.at[part * na + dp * 2 + core]
        rows[...] = total.astype(BF16)
        for chip in range(1, ndp):
            n = part * ndp + chip
            ag_copies[n] = send(rows, rows, ag_send.at[n], ag_recv.at[n], plane_id(chip))
        af_copies[part * ndp] = forward(part, 0)
    for part in range(parts):
        for chip in range(1, ndp):
            ag_copies[part * ndp + chip].wait_recv()
            af_copies[part * ndp + chip] = forward(part, chip)
    for copy in line_copies + core_copies:
        copy.wait_send()
    for copies in (pair_copies, rs_copies, gz_copies, ag_copies, af_copies):
        for copy in copies.values():
            copy.wait_send()
    loads[5].wait()
    loads[6].wait()
    for copy in af_copies.values():
        copy.wait_recv()
    norm = (BLK * nctx * ndp) ** (-0.5)
    for p in range(na):
        for part in range(parts):
            total = abuf[part * na + p].astype(F32) * norm
            dfirst, ufirst = p * wd + part * dpart, p * wu + part * upart
            step_down[:, dfirst : dfirst + dpart] += total[:, :dpart]
            step_up[:, ufirst : ufirst + upart] += total[:, dpart:]
    stores = [
        pltpu.make_async_copy(step_down, step_down_hbm, store_sem.at[1]),
        pltpu.make_async_copy(step_up, step_up_hbm, store_sem.at[2]),
    ]
    for copy in stores:
        copy.start()
    for copy in [att_store] + stores:
        copy.wait()


def hand_over(*refs):
    sources, targets, held = refs[:3], refs[3:6], refs[6:9]
    in_sem, out_sem = refs[9:]
    first, second = [], []
    for i in range(3):
        rows = sources[i].shape[0] // 2
        for j in range(2):
            part, n = pl.ds(j * rows, rows), 2 * i + j
            first.append(
                pltpu.make_async_copy(sources[i].at[part], held[i].at[part], in_sem.at[n])
            )
            second.append(
                pltpu.make_async_copy(held[i].at[part], targets[i].at[part], out_sem.at[n])
            )
    for copy in first:
        copy.start()
    for arrive, leave in zip(first, second):
        arrive.wait()
        leave.start()
    for copy in second:
        copy.wait()


def body(
    ndp,
    nctx,
    normed_layer_input,
    frozen_query_rows,
    projected_keys,
    projected_values,
    output_gradient,
    adapter_down,
    adapter_up,
    langevin_down_noise,
    langevin_up_noise,
    listed_key_blocks,
    head_live_slots,
):
    tok, width = normed_layer_input.shape[1:]
    qw, kvw = frozen_query_rows.shape[2], projected_keys.shape[2]
    rank = adapter_up.shape[0]
    heads = qw // HEAD_SIZE
    keys = nctx * tok
    nz, na = nctx // 2, ndp * 2
    parts = 1 if width % (256 * na) or qw % (256 * na) else 2
    piece = (width + qw) // (na * parts)
    early = 2 * heads * tok * keys * 4 <= 2**24
    per_step = 4 if early else 1
    any_spec = pl.BlockSpec(memory_space=pl.ANY)
    vmem_spec = pl.BlockSpec(memory_space=pltpu.VMEM)
    smem_spec = pl.BlockSpec(memory_space=pltpu.SMEM)
    dma = pltpu.SemaphoreType.DMA
    held_rows = (nz, heads * tok) if early else (1, 16)
    results = (
        jax.ShapeDtypeStruct((tok, qw), BF16),
        jax.ShapeDtypeStruct((rank, width), F32),
        jax.ShapeDtypeStruct((rank, qw), F32),
    )
    outputs = pl.pallas_call(
        functools.partial(kernel, ndp, nctx, parts, per_step, early),
        out_shape=results,
        in_specs=[any_spec] * 7 + [vmem_spec] * 3 + [smem_spec],
        out_specs=(any_spec,) * 3,
        scratch_shapes=[
            pltpu.VMEM((tok, width), BF16),
            pltpu.VMEM((tok, qw), BF16),
            pltpu.VMEM((tok, qw), BF16),
            pltpu.VMEM((nz, 2 * BLK, 2 * kvw), BF16),
            pltpu.VMEM((tok, qw), BF16),
            pltpu.VMEM((tok, qw), BF16),
            pltpu.VMEM((tok, qw), BF16),
            pltpu.VMEM((rank, width), F32),
            pltpu.VMEM((rank, qw), F32),
            pltpu.VMEM((heads, keys), F32),
            pltpu.VMEM(held_rows + (2 * BLK,), BF16),
            pltpu.VMEM(held_rows + (2 * BLK,), F32),
            pltpu.VMEM(held_rows + (2 * HEAD_SIZE,), F32),
            pltpu.VMEM(held_rows + (HEAD_SIZE,), F32),
            pltpu.VMEM((parts * na, rank, piece), F32),
            pltpu.VMEM((parts * na, rank, piece), BF16),
            pltpu.VMEM((parts * ndp, rank, piece), BF16),
            pltpu.VMEM((parts * ndp, rank, piece), BF16),
            pltpu.VMEM((parts * ndp, rank, piece), BF16),
            pltpu.VMEM((parts * nz, rank, piece), BF16),
            pltpu.VMEM((parts * na, rank, piece), BF16),
            dma((7,)),
            dma((3,)),
            dma((nz,)),
            dma((nz,)),
            dma((nz,)),
            dma((nz,)),
            dma((parts * ndp,)),
            dma((parts * ndp,)),
            dma((parts * ndp,)),
            dma((parts * ndp,)),
            dma((parts * nz,)),
            dma((parts * nz,)),
            dma((parts * ndp,)),
            dma((parts * ndp,)),
            dma((parts * ndp,)),
            dma((parts * ndp,)),
        ],
        compiler_params=pltpu.CompilerParams(
            collective_id=0,
            has_side_effects=True,
            vmem_limit_bytes=60 * 2**20,
        ),
        name="adapter_attention",
    )(
        normed_layer_input[0],
        frozen_query_rows[0],
        projected_keys[0],
        projected_values[0],
        output_gradient[0],
        langevin_down_noise.T,
        langevin_up_noise,
        adapter_down.T,
        adapter_up,
        listed_key_blocks.transpose(2, 1, 0),
        head_live_slots,
    )
    attended, step_down, step_up = pl.pallas_call(
        hand_over,
        out_shape=results,
        in_specs=[any_spec] * 3,
        out_specs=(any_spec,) * 3,
        scratch_shapes=[pltpu.VMEM(r.shape, r.dtype) for r in results] + [dma((6,)), dma((6,))],
        compiler_params=pltpu.CompilerParams(vmem_limit_bytes=60 * 2**20),
        name="hand_over",
    )(*outputs)
    return attended[None], step_down.T, step_up


def solution(mesh):
    rows = P("dp", "ctx", None)
    return jax.shard_map(
        functools.partial(body, mesh.shape["dp"], mesh.shape["ctx"]),
        mesh=mesh,
        in_specs=(rows,) * 5 + (P(),) * 6,
        out_specs=(rows, P(), P()),
        check_vma=False,
    )
```

```python
import functools

import jax
import jax.numpy as jnp
from jax import lax
from jax.experimental import pallas as pl
from jax.experimental.pallas import tpu as pltpu
from jax.sharding import PartitionSpec as P

HEAD_SIZE = 128
G = 8
BLK = 128
ADAPTER_GAIN = 2.0
MASK_VALUE = -1e30
LOG2E = 1.4426950408889634
MESH = pl.DeviceIdType.MESH
F32 = jnp.float32
BF16 = jnp.bfloat16


def dot_nt(a, b):
    return lax.dot_general(a, b, (((1,), (1,)), ((), ())), preferred_element_type=F32)


def dot_tn(a, b):
    return lax.dot_general(a, b, (((0,), (0,)), ((), ())), preferred_element_type=F32)


def dot_nn(a, b):
    return jnp.dot(a, b, preferred_element_type=F32)


def send(source, target, send_sem, recv_sem, device):
    copy = pltpu.make_async_remote_copy(
        src_ref=source,
        dst_ref=target,
        send_sem=send_sem,
        recv_sem=recv_sem,
        device_id=device,
        device_id_type=MESH,
    )
    copy.start()
    return copy


def kernel(
    ndp,
    nctx,
    parts,
    per_step,
    early,
    x_hbm,
    frozen_hbm,
    k_hbm,
    v_hbm,
    og_hbm,
    noise_down_hbm,
    noise_up_hbm,
    down_t,
    up,
    lists,
    live,
    att_hbm,
    step_down_hbm,
    step_up_hbm,
    x,
    frozen,
    og,
    kv,
    q,
    qg,
    att,
    step_down,
    step_up,
    bias,
    weights_buf,
    grads_buf,
    sums_buf,
    tops_buf,
    sbuf,
    pbuf,
    gbuf,
    rbuf,
    zbuf,
    abuf,
    load_sem,
    store_sem,
    z_send,
    z_recv,
    c_send,
    c_recv,
    p_send,
    p_recv,
    rs_send,
    rs_recv,
    gz_send,
    gz_recv,
    ag_send,
    ag_recv,
    af_send,
    af_recv,
):
    dp, ctx = lax.axis_index("dp"), lax.axis_index("ctx")
    nz, na = nctx // 2, ndp * 2
    z, core = lax.div(ctx, 2), lax.rem(ctx, 2)
    kvw = k_hbm.shape[1]
    width = x.shape[1]
    qw = q.shape[1]
    heads = qw // HEAD_SIZE
    wd, wu = width // na, qw // na
    keys = nctx * BLK

    own_rows = pl.ds(pl.multiple_of(core * BLK, BLK), BLK)

    def line(k):
        if nz & (nz - 1):
            return lax.rem(z + nz - k, nz)
        other, bit = z, 1
        while bit < nz:
            if k & bit:
                other = other + bit * (1 - 2 * lax.rem(lax.div(z, bit), 2))
            bit *= 2
        return other

    sibling = (dp, z * 2 + 1 - core)

    def plane_id(k):
        return (lax.rem(dp + k, ndp), ctx)

    def line_id(k):
        to = lax.rem(z + k, nz) if nz & (nz - 1) else line(k)
        return (dp, to * 2 + core)

    loads = []
    for i, (src, dst) in enumerate(
        (
            (k_hbm, kv.at[0, own_rows, pl.ds(0, kvw)]),
            (v_hbm, kv.at[0, own_rows, pl.ds(kvw, kvw)]),
            (x_hbm, x),
            (frozen_hbm, frozen),
            (og_hbm, og),
            (noise_down_hbm, step_down),
            (noise_up_hbm, step_up),
        )
    ):
        copy = pltpu.make_async_copy(src, dst, load_sem.at[i])
        copy.start()
        loads.append(copy)

    barrier = pltpu.get_barrier_semaphore()
    partners = [sibling]
    partners += [plane_id(k) for k in range(1, ndp)]
    partners += [line_id(k) for k in range(1, nz)]
    for partner in partners:
        pl.semaphore_signal(barrier, inc=1, device_id=partner, device_id_type=MESH)

    pl.semaphore_wait(barrier, len(partners))

    line_copies = []
    for k in range(1, nz):
        for i, source in enumerate((k_hbm, v_hbm)):
            target = kv.at[k, own_rows, pl.ds(i * kvw, kvw)]
            n = i * nz + k
            line_copies.append(send(source, target, z_send.at[n], z_recv.at[n], line_id(k)))

    def to_sibling(k):
        rows = kv.at[k, own_rows, :]
        return send(rows, rows, c_send.at[k], c_recv.at[k], sibling)

    loads[0].wait()
    loads[1].wait()
    core_copies = [to_sibling(0)]

    slots, nqb = lists.shape[:2]
    mine = lax.broadcasted_iota(jnp.int32, lists.shape, 1) == ctx
    local = jnp.sum(jnp.where(mine, lists[...].astype(F32), 0.0), axis=1)
    head_iota = lax.broadcasted_iota(jnp.int32, (1, heads), 1)
    live_row = jnp.zeros((1, heads), jnp.int32)
    for h in range(heads):
        live_row = jnp.where(head_iota == h, live[h], live_row)
    block_iota = lax.broadcasted_iota(jnp.int32, (nqb, heads), 0).astype(F32)
    count = jnp.zeros((nqb, heads), F32)
    for j in range(slots):
        listed = jnp.where(live_row > j, local[j : j + 1, :], -1.0)
        count += jnp.where(block_iota == listed, 1.0, 0.0)
    lane = lax.broadcasted_iota(jnp.int32, (1, keys), 1)
    held = jnp.zeros((1, keys), jnp.int32)
    for k in range(nz):
        held = jnp.where(lane // (2 * BLK) == k, line(k) * 2, held)
    held += (lane // BLK) % 2
    spread = jnp.where(lax.broadcasted_iota(jnp.int32, (nqb, keys), 0) == held, 1.0, 0.0)
    count = dot_tn(count, spread)
    bias[...] = jnp.where(count > 0.5, jnp.log(jnp.maximum(count, 1.0)) * LOG2E, MASK_VALUE)

    loads[2].wait()
    low_rank = dot_nt(x[...], down_t[...]).astype(BF16)
    loads[3].wait()
    q[...] = (frozen[...].astype(F32) + ADAPTER_GAIN * dot_nn(low_rank, up[...])).astype(BF16)

    loads[4].wait()
    scaling = HEAD_SIZE ** (-0.5)
    pair = 2 * BLK

    def stacked(ref, first, number):
        return jnp.concatenate(
            [
                ref[:, pl.ds(pl.multiple_of((first + j) * HEAD_SIZE, HEAD_SIZE), HEAD_SIZE)]
                for j in range(number)
            ],
            axis=0,
        )

    def scores_of(k):
        def group_step(group, carry):
            kcols = pl.ds(pl.multiple_of(group * HEAD_SIZE, HEAD_SIZE), HEAD_SIZE)
            vcols = pl.ds(pl.multiple_of(kvw + group * HEAD_SIZE, HEAD_SIZE), HEAD_SIZE)
            rows = pl.ds(pl.multiple_of(group * G * BLK, G * BLK), G * BLK)
            scores = dot_nt(stacked(q, group * G, G), kv[k, :, kcols])
            grads_buf[k, rows, :] = dot_nt(stacked(og, group * G, G), kv[k, :, vcols])
            group_bias = bias[pl.ds(pl.multiple_of(group * G, G), G), k * pair : (k + 1) * pair]
            all_weights = []
            for j in range(G):
                head_rows = pl.ds(pl.multiple_of((group * G + j) * BLK, BLK), BLK)
                head_scores = scores[j * BLK : (j + 1) * BLK] * (scaling * LOG2E)
                head_scores += group_bias[j : j + 1]
                top = jnp.max(head_scores, axis=-1, keepdims=True)
                tops_buf[k, head_rows, :] = jnp.broadcast_to(top, (BLK, HEAD_SIZE))
                all_weights.append(jnp.exp2(head_scores - top).astype(BF16))
            weights = jnp.concatenate(all_weights, axis=0)
            weights_buf[k, rows, :] = weights
            values = jnp.concatenate([kv[k, :, vcols], jnp.ones((pair, HEAD_SIZE), BF16)], axis=1)
            sums_buf[k, rows, :] = dot_nn(weights, values)
            return carry

        lax.fori_loop(0, heads // G, group_step, 0)

    for k in range(nz):
        if k > 0:
            for copy in line_copies[2 * k - 2 : 2 * k]:
                copy.wait_recv()
            core_copies.append(to_sibling(k))
        if early:
            core_copies[k].wait_recv()
            scores_of(k)
    if not early:
        for copy in core_copies:
            copy.wait_recv()

    def finish_step(i, carry):
        first = i * per_step
        kcols = pl.ds(pl.multiple_of(first // G * HEAD_SIZE, HEAD_SIZE), HEAD_SIZE)
        score_grads = [[] for _ in range(nz)]
        factors, scales = [], []
        for j in range(per_step):
            rows = pl.ds(pl.multiple_of((first + j) * BLK, BLK), BLK)
            cols = pl.ds(pl.multiple_of((first + j) * HEAD_SIZE, HEAD_SIZE), HEAD_SIZE)
            tops = [tops_buf[k, rows, :] for k in range(nz)]
            top = functools.reduce(jnp.maximum, tops)
            factor = [jnp.exp2(t - top) for t in tops]
            attended, total = 0.0, 0.0
            for k in range(nz):
                attended += factor[k] * sums_buf[k, rows, :HEAD_SIZE]
                total += factor[k] * sums_buf[k, rows, HEAD_SIZE:]
            inverse = 1.0 / total
            attended = attended * inverse
            att[:, cols] = attended.astype(BF16)
            inner = jnp.sum(attended * og[:, cols].astype(F32), axis=-1, keepdims=True)
            for k in range(nz):
                weights = weights_buf[k, rows, :].astype(F32)
                score_grads[k].append((weights * (grads_buf[k, rows, :] - inner)).astype(BF16))
            factors.append(factor)
            scales.append(inverse * scaling)
        parts = [
            dot_nn(jnp.concatenate(score_grads[k], axis=0), kv[k, :, kcols]) for k in range(nz)
        ]
        for j in range(per_step):
            cols = pl.ds(pl.multiple_of((first + j) * HEAD_SIZE, HEAD_SIZE), HEAD_SIZE)
            query_grad = 0.0
            for k in range(nz):
                query_grad += factors[j][k] * parts[k][j * BLK : (j + 1) * BLK]
            qg[:, cols] = (query_grad * scales[j]).astype(BF16)
        return carry

    def head_step(i, carry):
        first = i * per_step
        group = first // G
        kcols = pl.ds(pl.multiple_of(group * HEAD_SIZE, HEAD_SIZE), HEAD_SIZE)
        vcols = pl.ds(pl.multiple_of(kvw + group * HEAD_SIZE, HEAD_SIZE), HEAD_SIZE)
        key_rows = kv[:, :, kcols].reshape(keys, HEAD_SIZE)
        value_rows = kv[:, :, vcols].reshape(keys, HEAD_SIZE)
        all_weights, all_grads, all_inverse = [], [], []
        for j in range(per_step):
            h = first + j
            cols = pl.ds(pl.multiple_of(h * HEAD_SIZE, HEAD_SIZE), HEAD_SIZE)
            scores = dot_nt(q[:, cols], key_rows)
            weight_grad = dot_nt(og[:, cols], value_rows)
            scores = scores * (scaling * LOG2E) + bias[pl.ds(h, 1), :]
            weights = jnp.exp2(scores - jnp.max(scores, axis=-1, keepdims=True))
            inverse = 1.0 / jnp.sum(weights, axis=-1, keepdims=True)
            inner = jnp.sum(weights * weight_grad, axis=-1, keepdims=True) * inverse
            all_weights.append(weights.astype(BF16))
            all_grads.append((weights * (weight_grad - inner)).astype(BF16))
            all_inverse.append(inverse)
        attended = dot_nn(jnp.concatenate(all_weights, axis=0), value_rows)
        query_grad = dot_nn(jnp.concatenate(all_grads, axis=0), key_rows)
        for j in range(per_step):
            cols = pl.ds(pl.multiple_of((first + j) * HEAD_SIZE, HEAD_SIZE), HEAD_SIZE)
            rows = slice(j * BLK, (j + 1) * BLK)
            att[:, cols] = (attended[rows] * all_inverse[j]).astype(BF16)
            qg[:, cols] = (query_grad[rows] * (all_inverse[j] * scaling)).astype(BF16)
        return carry

    lax.fori_loop(0, heads // per_step, finish_step if early else head_step, 0)
    att_store = pltpu.make_async_copy(att, att_hbm, store_sem.at[0])
    att_store.start()

    low_grad = (ADAPTER_GAIN * dot_nt(qg[...], up[...])).astype(BF16)

    dpart, upart = wd // parts, wu // parts

    def chunk(chip, part, kind):
        p = lax.rem(dp + chip, ndp) * 2 + kind
        dcols = pl.ds(pl.multiple_of(p * wd + part * dpart, 128), dpart)
        ucols = pl.ds(pl.multiple_of(p * wu + part * upart, 128), upart)
        part_down = dot_tn(low_grad, x[:, dcols])
        part_up = ADAPTER_GAIN * dot_tn(low_rank, qg[:, ucols])
        return jnp.concatenate([part_down, part_up], axis=1)

    order = [(part, chip) for part in range(parts) for chip in list(range(1, ndp)) + [0]]
    pair_copies, rs_copies, gz_copies, ag_copies, af_copies = {}, {}, {}, {}, {}
    for part, chip in order:
        n = part * ndp + chip
        sbuf[n] = chunk(chip, part, 1 - core).astype(BF16)
        pair_copies[n] = send(sbuf.at[n], pbuf.at[n], p_send.at[n], p_recv.at[n], sibling)
    sums = {}
    for part, chip in order:
        n = part * ndp + chip
        own = chunk(chip, part, core)
        pair_copies[n].wait_recv()
        own += pbuf[n].astype(F32)
        if chip == 0:
            sums[part] = own
        else:
            gbuf[n] = own.astype(BF16)
            rs_copies[n] = send(gbuf.at[n], rbuf.at[n], rs_send.at[n], rs_recv.at[n], plane_id(chip))
    for part in range(parts):
        total = sums[part]
        for chip in range(1, ndp):
            n = part * ndp + chip
            rs_copies[n].wait_recv()
            total += rbuf[n].astype(F32)
        slot = part * nz + z
        zbuf[slot] = total.astype(BF16)
        for k in range(1, nz):
            n = part * nz + k
            gz_copies[n] = send(zbuf.at[slot], zbuf.at[slot], gz_send.at[n], gz_recv.at[n], line_id(k))

    def forward(part, chip):
        n = part * ndp + chip
        rows = abuf.at[part * na + lax.rem(dp + ndp - chip, ndp) * 2 + core]
        return send(rows, rows, af_send.at[n], af_recv.at[n], sibling)

    for part in range(parts):
        for k in range(1, nz):
            gz_copies[part * nz + k].wait_recv()
        total = zbuf[part * nz].astype(F32)
        for i in range(1, nz):
            total += zbuf[part * nz + i].astype(F32)
        rows = abuf.at[part * na + dp * 2 + core]
        rows[...] = total.astype(BF16)
        for chip in range(1, ndp):
            n = part * ndp + chip
            ag_copies[n] = send(rows, rows, ag_send.at[n], ag_recv.at[n], plane_id(chip))
        af_copies[part * ndp] = forward(part, 0)
    for part in range(parts):
        for chip in range(1, ndp):
            ag_copies[part * ndp + chip].wait_recv()
            af_copies[part * ndp + chip] = forward(part, chip)
    for copy in line_copies + core_copies:
        copy.wait_send()
    for copies in (pair_copies, rs_copies, gz_copies, ag_copies, af_copies):
        for copy in copies.values():
            copy.wait_send()
    loads[5].wait()
    loads[6].wait()
    for copy in af_copies.values():
        copy.wait_recv()
    norm = (BLK * nctx * ndp) ** (-0.5)
    for p in range(na):
        for part in range(parts):
            total = abuf[part * na + p].astype(F32) * norm
            dfirst, ufirst = p * wd + part * dpart, p * wu + part * upart
            step_down[:, dfirst : dfirst + dpart] += total[:, :dpart]
            step_up[:, ufirst : ufirst + upart] += total[:, dpart:]
    stores = [
        pltpu.make_async_copy(step_down, step_down_hbm, store_sem.at[1]),
        pltpu.make_async_copy(step_up, step_up_hbm, store_sem.at[2]),
    ]
    for copy in stores:
        copy.start()
    for copy in [att_store] + stores:
        copy.wait()


def hand_over(*refs):
    sources, targets, held = refs[:3], refs[3:6], refs[6:9]
    in_sem, out_sem = refs[9:]
    first, second = [], []
    for i in range(3):
        rows = sources[i].shape[0] // 2
        for j in range(2):
            part, n = pl.ds(j * rows, rows), 2 * i + j
            first.append(
                pltpu.make_async_copy(sources[i].at[part], held[i].at[part], in_sem.at[n])
            )
            second.append(
                pltpu.make_async_copy(held[i].at[part], targets[i].at[part], out_sem.at[n])
            )
    for copy in first:
        copy.start()
    for arrive, leave in zip(first, second):
        arrive.wait()
        leave.start()
    for copy in second:
        copy.wait()


def body(
    ndp,
    nctx,
    normed_layer_input,
    frozen_query_rows,
    projected_keys,
    projected_values,
    output_gradient,
    adapter_down,
    adapter_up,
    langevin_down_noise,
    langevin_up_noise,
    listed_key_blocks,
    head_live_slots,
):
    tok, width = normed_layer_input.shape[1:]
    qw, kvw = frozen_query_rows.shape[2], projected_keys.shape[2]
    rank = adapter_up.shape[0]
    heads = qw // HEAD_SIZE
    keys = nctx * tok
    nz, na = nctx // 2, ndp * 2
    parts = 1 if width % (256 * na) or qw % (256 * na) else 2
    piece = (width + qw) // (na * parts)
    early = 2 * heads * tok * keys * 4 <= 2**24
    per_step = 4 if early else 1
    any_spec = pl.BlockSpec(memory_space=pl.ANY)
    vmem_spec = pl.BlockSpec(memory_space=pltpu.VMEM)
    smem_spec = pl.BlockSpec(memory_space=pltpu.SMEM)
    dma = pltpu.SemaphoreType.DMA
    held_rows = (nz, heads * tok) if early else (1, 16)
    results = (
        jax.ShapeDtypeStruct((tok, qw), BF16),
        jax.ShapeDtypeStruct((rank, width), F32),
        jax.ShapeDtypeStruct((rank, qw), F32),
    )
    outputs = pl.pallas_call(
        functools.partial(kernel, ndp, nctx, parts, per_step, early),
        out_shape=results,
        in_specs=[any_spec] * 7 + [vmem_spec] * 3 + [smem_spec],
        out_specs=(any_spec,) * 3,
        scratch_shapes=[
            pltpu.VMEM((tok, width), BF16),
            pltpu.VMEM((tok, qw), BF16),
            pltpu.VMEM((tok, qw), BF16),
            pltpu.VMEM((nz, 2 * BLK, 2 * kvw), BF16),
            pltpu.VMEM((tok, qw), BF16),
            pltpu.VMEM((tok, qw), BF16),
            pltpu.VMEM((tok, qw), BF16),
            pltpu.VMEM((rank, width), F32),
            pltpu.VMEM((rank, qw), F32),
            pltpu.VMEM((heads, keys), F32),
            pltpu.VMEM(held_rows + (2 * BLK,), BF16),
            pltpu.VMEM(held_rows + (2 * BLK,), F32),
            pltpu.VMEM(held_rows + (2 * HEAD_SIZE,), F32),
            pltpu.VMEM(held_rows + (HEAD_SIZE,), F32),
            pltpu.VMEM((parts * ndp, rank, piece), BF16),
            pltpu.VMEM((parts * ndp, rank, piece), BF16),
            pltpu.VMEM((parts * ndp, rank, piece), BF16),
            pltpu.VMEM((parts * ndp, rank, piece), BF16),
            pltpu.VMEM((parts * nz, rank, piece), BF16),
            pltpu.VMEM((parts * na, rank, piece), BF16),
            dma((7,)),
            dma((3,)),
            dma((2 * nz,)),
            dma((2 * nz,)),
            dma((nz,)),
            dma((nz,)),
            dma((parts * ndp,)),
            dma((parts * ndp,)),
            dma((parts * ndp,)),
            dma((parts * ndp,)),
            dma((parts * nz,)),
            dma((parts * nz,)),
            dma((parts * ndp,)),
            dma((parts * ndp,)),
            dma((parts * ndp,)),
            dma((parts * ndp,)),
        ],
        compiler_params=pltpu.CompilerParams(
            collective_id=0,
            has_side_effects=True,
            vmem_limit_bytes=60 * 2**20,
        ),
        name="adapter_attention",
    )(
        normed_layer_input[0],
        frozen_query_rows[0],
        projected_keys[0],
        projected_values[0],
        output_gradient[0],
        langevin_down_noise.T,
        langevin_up_noise,
        adapter_down.T,
        adapter_up,
        listed_key_blocks.transpose(2, 1, 0),
        head_live_slots,
    )
    attended, step_down, step_up = pl.pallas_call(
        hand_over,
        out_shape=results,
        in_specs=[any_spec] * 3,
        out_specs=(any_spec,) * 3,
        scratch_shapes=[pltpu.VMEM(r.shape, r.dtype) for r in results] + [dma((6,)), dma((6,))],
        compiler_params=pltpu.CompilerParams(vmem_limit_bytes=60 * 2**20),
        name="hand_over",
    )(*outputs)
    return attended[None], step_down.T, step_up


def solution(mesh):
    rows = P("dp", "ctx", None)
    return jax.shard_map(
        functools.partial(body, mesh.shape["dp"], mesh.shape["ctx"]),
        mesh=mesh,
        in_specs=(rows,) * 5 + (P(),) * 6,
        out_specs=(rows, P(), P()),
        check_vma=False,
    )
```
